128 devices in a mesh: dp: 16 (over x, z_hi, core), expert: 8 (over y, z_lo).
Axes of the slice: x: 4, y: 4, z: 4 (z_hi: 2, z_lo: 2; z = z_hi * 2 + z_lo), core: 2. Of those that a mesh axis runs over, the one named last changes fastest.
Arguments:
- tokens: bfloat16 [16384, 2880], P(('dp', 'expert')), may hold values from -6 to 6
- expert_ids: int32 [16384, 4], P(('dp', 'expert')), may hold values from 0 to 63, all different within a row
- gate_raw: float32 [16384, 4], P(('dp', 'expert')), may hold values from 0.1 to 1
- overflow_shift: int32 [16384, 4], P(('dp', 'expert')), may hold values from 1 to 63
- limits: int32 [64], replicated, may hold values from 6 to 12, as said below
- gate_w: bfloat16 [128, 2880, 768], P(('dp', 'expert')), may hold values from -0.109375 to 0.109375
- up_w: bfloat16 [128, 2880, 768], P(('dp', 'expert')), may hold values from -0.109375 to 0.109375
- down_w: bfloat16 [128, 768, 2880], P(('dp', 'expert')), may hold values from -0.15625 to 0.15625
- context: bfloat16 [16384, 4096], P('dp', 'expert'), may hold values from -6 to 6
- out_grad: bfloat16 [16384, 2880], P(('dp', 'expert')), may hold values from -0.059814453 to 0.059814453
Outputs:
- mixed: bfloat16 [16384, 2880], P(('dp', 'expert'))
- proj_grad: float32 [4096, 2880], P('expert')
The draws below stay inside these ranges and needn't reach their ends.
Inputs may be any that keep to these rules, and one draw needn't show every extreme that they name: `limits`: each expert has between 6 and 12 first-choice slots.
All inputs are finite; a program needn't handle non-finite values.
Results may differ from the reference program's by a relative error of at most 0.023.
Values may be sent and summed in bfloat16 or wider, within the bound.
No kernel may reach another device: no remote copies, remote signals or barrier semaphores. Data moves between devices by JAX's collectives and lax.ppermute only.
A program may use at most 192 MiB of HBM per device.

```python
import math
import jax
import jax.numpy as jnp
from jax import lax

D = 2880
FF = 1536
TOPK = 4
HEADS = 64
HD = 64
TOK_DEV = 128
EXPERTS = 64
TOKENS = 16384
CAP = 12


def draw_limits(key, part):
    key = jax.random.fold_in(key, 11)
    keys = jax.random.split(key, 3)
    values = jax.random.randint(keys[0], (EXPERTS,), CAP // 2, CAP + 1, dtype=jnp.int32)
    top_at = jax.random.randint(keys[1], (), 0, EXPERTS, dtype=jnp.int32)
    low_at = (top_at + 1 + jax.random.randint(keys[2], (), 0, EXPERTS - 1, dtype=jnp.int32)) % EXPERTS
    places = jnp.arange(EXPERTS, dtype=jnp.int32)
    values = jnp.where(places == top_at, CAP, values)
    values = jnp.where(places == low_at, CAP // 2, values)
    return values


def set_ends(values, key, smallest, largest):
    extent = values.shape
    index_at = [jax.random.randint(jax.random.fold_in(key, axis), (), 0, extent[axis]) for axis in range(len(extent))]
    values = values.at[tuple(index_at)].set(smallest)
    longest = extent.index(max(extent))
    index_at[longest] = (index_at[longest] + 1) % extent[longest]
    return values.at[tuple(index_at)].set(largest)


def level_of(rng, dims, pieces, low, top_value):
    def one(axis_at, shards_of):
        steps = jax.random.uniform(jax.random.fold_in(jax.random.fold_in(rng, 6), axis_at), (shards_of,), jnp.float32, low / len(pieces), top_value / len(pieces))
        return jnp.repeat(jnp.exp(steps), dims[axis_at] // shards_of).reshape((-1,) + (1,) * (len(dims) - axis_at - 1))

    factor_of = one(*pieces[0])
    for cut in pieces[1:]:
        factor_of = factor_of * one(*cut)
    return factor_of


def picks_of(own_key, rows, number_of, top, lift):
    ranking = jax.random.permutation(jax.random.fold_in(own_key, 1), number_of)
    pull = ranking
    for power in range(3):
        pull = pull * pull // number_of
    pull = pull * lift // number_of
    lots = jax.random.randint(jax.random.fold_in(own_key, 2), (rows, number_of), 0, 4096) + pull
    sure = jax.random.permutation(jax.random.fold_in(own_key, 3), rows)[jnp.arange(number_of) % rows]
    lots = jnp.where(jnp.arange(rows)[:, None] == sure[None, :], 1 << 14, lots)
    score = lots * number_of + jnp.arange(number_of)
    return lax.top_k(score.astype(jnp.int32), top)[1].astype(jnp.int32)


def gaussian(stream_key, shape, width, reach, cuts=(), held_as=jnp.bfloat16):
    values = jax.random.normal(stream_key, shape, jnp.float32) * width
    if len(cuts) > 0:
        values = level_of(stream_key, shape, cuts, -0.22, 0.18) * values
    return jnp.clip(values, min=-reach, max=reach).astype(held_as)


def setup_inputs(seed: int = 0) -> dict:
    arg_keys = jax.random.split(jax.random.key(seed), 11)
    tokens = gaussian(arg_keys[0], (TOKENS, D), 1.0, 6.0, ((0, 128),))
    expert_ids = picks_of(arg_keys[1], TOKENS, EXPERTS, TOPK, 1024)
    gate_raw = jnp.clip(jnp.exp(math.log(1.0) - 2.3025851 * jax.random.uniform(arg_keys[2], (TOKENS, TOPK), jnp.float32) ** level_of(arg_keys[2], (TOKENS, TOPK), ((0, 128),), -0.2, 0.2)), 0.1, 1.0)
    overflow_shift = set_ends(jax.random.randint(arg_keys[3], (TOKENS, TOPK), 1, EXPERTS), jax.random.fold_in(arg_keys[3], 1), 1, EXPERTS - 1).astype(jnp.int32)
    limits = draw_limits(jax.random.fold_in(arg_keys[10], 71), 0)
    gate_w = gaussian(arg_keys[5], (2 * EXPERTS, D, FF // 2), D ** -0.5, 0.109375, ((0, 128),))
    up_w = gaussian(arg_keys[6], (2 * EXPERTS, D, FF // 2), D ** -0.5, 0.109375, ((0, 128),))
    down_w = gaussian(arg_keys[7], (2 * EXPERTS, FF // 2, D), FF ** -0.5, 0.15625, ((0, 128),))
    context = gaussian(arg_keys[8], (TOKENS, HEADS * HD), 1.0, 6.0, ((0, 16), (1, 8)))
    out_grad = gaussian(arg_keys[9], (TOKENS, D), 0.01, 0.059814453, ((0, 128),))
    return {"tokens": tokens, "expert_ids": expert_ids, "gate_raw": gate_raw, "overflow_shift": overflow_shift, "limits": limits, "gate_w": gate_w, "up_w": up_w, "down_w": down_w, "context": context, "out_grad": out_grad}


def place_slots(expert_ids, overflow_shift, limits, capacity):
    experts = limits.shape[0]
    flat_ids = expert_ids.reshape(-1)
    shifts = overflow_shift.reshape(-1)
    labels = jnp.arange(experts, dtype=jnp.int32)
    first_hot = (flat_ids[:, None] == labels[None, :]).astype(jnp.int32)
    first_before = jnp.cumsum(first_hot, axis=0, dtype=jnp.int32) - first_hot
    first_rank = jnp.sum(first_before * first_hot, axis=1, dtype=jnp.int32)
    first_limit = jnp.sum(first_hot * limits[None, :], axis=1, dtype=jnp.int32)
    spilled = first_rank >= first_limit
    second = (flat_ids + shifts) % experts
    second_any = (second[:, None] == labels[None, :]).astype(jnp.int32)
    second_hot = second_any * spilled.astype(jnp.int32)[:, None]
    second_before = jnp.cumsum(second_hot, axis=0, dtype=jnp.int32) - second_hot
    second_rank = jnp.sum(second_before * second_hot, axis=1, dtype=jnp.int32)
    second_limit = jnp.sum(second_any * limits[None, :], axis=1, dtype=jnp.int32)
    target = jnp.where(spilled, second, flat_ids)
    slot_index = jnp.where(spilled, second_limit + second_rank, first_rank)
    return target, slot_index, slot_index < capacity


def expert_part(token_rows, gate_half, up_half, down_half):
    gating = jnp.dot(token_rows, gate_half, preferred_element_type=jnp.float32)
    upward = jnp.dot(token_rows, up_half, preferred_element_type=jnp.float32)
    active = ((upward + 1.0) * gating * jax.nn.sigmoid(1.702 * gating)).astype(jnp.bfloat16)
    return jnp.dot(active, down_half, preferred_element_type=jnp.float32).astype(jnp.bfloat16)


def reference(tokens, expert_ids, gate_raw, overflow_shift, limits, gate_w, up_w, down_w, context, out_grad):
    group_count = TOKENS // TOK_DEV
    assign_count = TOK_DEV * TOPK

    def one_group(group_ids, group_shifts):
        return place_slots(group_ids, group_shifts, limits, CAP)

    target, slot_index, is_kept = jax.vmap(one_group)(
        expert_ids.reshape(group_count, TOK_DEV, TOPK), overflow_shift.reshape(group_count, TOK_DEV, TOPK))
    where_to = jnp.where(is_kept, target * CAP + slot_index, EXPERTS * CAP)

    def fill_lookup(destination):
        empty = jnp.full((EXPERTS * CAP,), -1, jnp.int32)
        return empty.at[destination].set(jnp.arange(assign_count, dtype=jnp.int32), mode="drop")

    lookup = jax.vmap(fill_lookup)(where_to)
    gate_share = gate_raw / jnp.sum(gate_raw, axis=1, keepdims=True)
    share_flat = gate_share.reshape(group_count, assign_count)
    group_base = (jnp.arange(group_count, dtype=jnp.int32) * TOK_DEV)[:, None]

    def one_expert(totals, expert_index):
        picked = lax.dynamic_slice_in_dim(lookup, expert_index * CAP, CAP, 1)
        usable = picked >= 0
        clipped = jnp.maximum(picked, 0)
        token_at = group_base + clipped // TOPK
        token_rows = jnp.where(usable[:, :, None], tokens[token_at], jnp.zeros((), jnp.bfloat16))
        token_rows = token_rows.reshape(group_count * CAP, D)
        merged = jnp.zeros((group_count * CAP, D), jnp.float32)
        for which_half in range(2):
            index = 2 * expert_index + which_half
            merged = merged + expert_part(token_rows, gate_w[index], up_w[index], down_w[index]).astype(jnp.float32)
        weight = jnp.where(usable, jnp.take_along_axis(share_flat, clipped, axis=1), 0.0)
        totals = totals.at[token_at.reshape(-1)].add(weight.reshape(-1, 1) * merged)
        return totals, None

    totals, _ = lax.scan(one_expert, jnp.zeros((TOKENS, D), jnp.float32), jnp.arange(EXPERTS, dtype=jnp.int32))
    mixed = totals.astype(jnp.bfloat16)
    proj_grad = jnp.dot(context.T, out_grad, preferred_element_type=jnp.float32)
    return mixed, proj_grad
```

```python
import functools

import jax
import jax.numpy as jnp
from jax import lax
from jax.experimental import pallas as pl
from jax.experimental.pallas import tpu as pltpu
from jax.sharding import Mesh, PartitionSpec as P

CAP = 12
BF = jnp.bfloat16
F32 = jnp.float32
NT = (((1,), (1,)), ((), ()))


def place(ids, shifts, lim):
    label = lax.broadcasted_iota(jnp.int32, (64, 128), 0)
    earlier = (
        lax.broadcasted_iota(jnp.int32, (128, 128), 0)
        < lax.broadcasted_iota(jnp.int32, (128, 128), 1)
    ).astype(F32).astype(BF)
    rows = [ids[k : k + 1, :] for k in range(4)]
    hots = [(r == label).astype(F32) for r in rows]
    hot = hots[0] + hots[1] + hots[2] + hots[3]
    before = jnp.dot(hot.astype(BF), earlier, preferred_element_type=F32)
    spilled, seconds, second_hots, first_ranks = [], [], [], []
    for k in range(4):
        rank = jnp.sum(before * hots[k], axis=0, keepdims=True)
        limit = jnp.sum(lim * hots[k], axis=0, keepdims=True)
        spill = rank >= limit
        second = (rows[k] + shifts[k : k + 1, :]) & 63
        first_ranks.append(rank)
        spilled.append(spill)
        seconds.append(second)
        second_hots.append((second == label).astype(F32))
    spill_hots = [h * s.astype(F32) for h, s in zip(second_hots, spilled)]
    total = spill_hots[0] + spill_hots[1] + spill_hots[2] + spill_hots[3]
    run = jnp.dot(total.astype(BF), earlier, preferred_element_type=F32)
    out = []
    for k in range(4):
        rank = jnp.sum(run * second_hots[k], axis=0, keepdims=True)
        run = run + spill_hots[k]
        limit = jnp.sum(lim * second_hots[k], axis=0, keepdims=True)
        slot = jnp.where(spilled[k], limit + rank, first_ranks[k]).astype(jnp.int32)
        target = jnp.where(spilled[k], seconds[k], rows[k])
        out.append((target, slot, slot < CAP))
    return out


def local_rows(places, core, side):
    out = []
    for target, slot, kept in places:
        mine = kept & (((target >> 2) & 1) == core)
        index = (target >> 3) * 4 + (target & 3)
        out.append(jnp.where(mine, index * 24 + slot + side * CAP, -1))
    return out


def dispatch_kernel(own_ref, sib_ref, mo_ref, ms_ref, lim_ref, core_ref, out_ref, rows_ref, hot_ref, tok_ref):
    step = pl.program_id(0)

    @pl.when(step == 0)
    def _():
        core = core_ref[0]
        tok_ref[:, :128] = own_ref[...]
        tok_ref[:, 128:] = sib_ref[...]
        slot_of = lax.broadcasted_iota(jnp.int32, (768, 128), 0)
        for side, m_ref in enumerate((mo_ref, ms_ref)):
            m = m_ref[...]
            ids = m[0:4].astype(jnp.int32)
            shifts = m[4:8].astype(jnp.int32)
            rows = local_rows(place(ids, shifts, lim_ref[...]), core, side)
            hot = (rows[0] == slot_of) | (rows[1] == slot_of) | (rows[2] == slot_of) | (rows[3] == slot_of)
            hot_ref[:, 128 * side : 128 * side + 128] = hot.astype(F32).astype(BF)
            for k in range(4):
                rows_ref[4 * side + k : 4 * side + k + 1, :] = rows[k]

    part = hot_ref[pl.ds(pl.multiple_of(step * 192, 192), 192), :]
    got = lax.dot_general(part, tok_ref[...], NT, preferred_element_type=F32).astype(BF)
    out_ref[0] = got
    out_ref[1] = got


def dispatch(tok, sib_tok, meta, sib_meta, lim, core):
    vm = pl.BlockSpec(memory_space=pltpu.VMEM)
    return pl.pallas_call(
        dispatch_kernel,
        grid=(4,),
        in_specs=[vm, vm, vm, vm, vm, pl.BlockSpec(memory_space=pltpu.SMEM)],
        out_specs=[
            pl.BlockSpec((2, 192, 2880), lambda i: (0, i, 0)),
            pl.BlockSpec((8, 128), lambda i: (0, 0)),
        ],
        out_shape=[
            jax.ShapeDtypeStruct((2, 768, 2880), BF),
            jax.ShapeDtypeStruct((8, 128), jnp.int32),
        ],
        scratch_shapes=[pltpu.VMEM((768, 256), BF), pltpu.VMEM((2880, 256), BF)],
        compiler_params=pltpu.CompilerParams(vmem_limit_bytes=40 << 20),
        cost_estimate=pl.CostEstimate(flops=2 * 768 * 256 * 2880, bytes_accessed=11_000_000, transcendentals=0),
        name="dispatch",
    )(tok, sib_tok, meta, sib_meta, lim, core)


def ffn_kernel(x_ref, g_hbm, u_hbm, d_hbm, out_ref, g_ref, u_ref, d_ref, sems):
    step = pl.program_id(0)
    copies = [
        pltpu.make_async_copy(g_hbm.at[0], g_ref, sems.at[0]),
        pltpu.make_async_copy(u_hbm.at[0], u_ref, sems.at[1]),
        pltpu.make_async_copy(d_hbm, d_ref, sems.at[2]),
    ]

    @pl.when(step == 0)
    def _():
        for c in copies:
            c.start()
        copies[0].wait()

    x = x_ref[...]
    gating = jnp.dot(x, g_ref[...], preferred_element_type=F32)

    @pl.when(step == 0)
    def _():
        copies[1].wait()

    upward = jnp.dot(x, u_ref[...], preferred_element_type=F32)
    active = ((upward + 1.0) * gating * jax.nn.sigmoid(1.702 * gating)).astype(BF)

    @pl.when(step == 0)
    def _():
        copies[2].wait()

    out_ref[...] = lax.dot_general(active, d_ref[...], NT, preferred_element_type=F32).astype(BF)


def ffn(x, g, u, d_t, rows=384):
    count = x.shape[0]
    hbm = pl.BlockSpec(memory_space=pl.ANY)
    return pl.pallas_call(
        ffn_kernel,
        grid=(count // rows,),
        in_specs=[pl.BlockSpec((rows, 2880), lambda i: (i, 0)), hbm, hbm, hbm],
        out_specs=pl.BlockSpec((rows, 2880), lambda i: (i, 0)),
        out_shape=jax.ShapeDtypeStruct((count, 2880), BF),
        scratch_shapes=[
            pltpu.VMEM((2880, 768), BF),
            pltpu.VMEM((2880, 768), BF),
            pltpu.VMEM((2880, 768), BF),
            pltpu.SemaphoreType.DMA((3,)),
        ],
        compiler_params=pltpu.CompilerParams(vmem_limit_bytes=48 << 20),
        cost_estimate=pl.CostEstimate(
            flops=6 * count * 2880 * 768, bytes_accessed=13_300_000 + count * 2880 * 4, transcendentals=count * 768
        ),
        name="ffn",
    )(x, g, u, d_t)


def combine_kernel(y_ref, rows_ref, mo_ref, ms_ref, own_ref, sib_ref, w_ref, acc_ref):
    step = pl.program_id(0)

    @pl.when(step == 0)
    def _():
        slot_of = lax.broadcasted_iota(jnp.int32, (768, 128), 0)
        for side, m_ref in enumerate((mo_ref, ms_ref)):
            raw = m_ref[8:12]
            share = raw / jnp.sum(raw, axis=0, keepdims=True)
            w = jnp.zeros((768, 128), F32)
            for k in range(4):
                w = w + jnp.where(rows_ref[4 * side + k : 4 * side + k + 1, :] == slot_of, share[k : k + 1], 0.0)
            wt = w.T.astype(BF)
            for b in range(4):
                w_ref[b, 128 * side : 128 * side + 128, :] = wt[:, 192 * b : 192 * b + 192]
        acc_ref[...] = jnp.zeros_like(acc_ref)

    w = w_ref[step]
    acc_ref[...] += jnp.dot(w, y_ref[0], preferred_element_type=F32) + jnp.dot(
        w, y_ref[1], preferred_element_type=F32
    )

    @pl.when(step == 3)
    def _():
        own_ref[...] = acc_ref[:128, :].T
        sib_ref[...] = acc_ref[128:, :].T.astype(BF)


def combine(y, rows, meta, sib_meta):
    vm = pl.BlockSpec(memory_space=pltpu.VMEM)
    return pl.pallas_call(
        combine_kernel,
        grid=(4,),
        in_specs=[pl.BlockSpec((2, 192, 2880), lambda i: (0, i, 0)), vm, vm, vm],
        out_specs=[pl.BlockSpec((2880, 128), lambda i: (0, 0))] * 2,
        out_shape=[jax.ShapeDtypeStruct((2880, 128), F32), jax.ShapeDtypeStruct((2880, 128), BF)],
        scratch_shapes=[pltpu.VMEM((4, 256, 192), BF), pltpu.VMEM((256, 2880), F32)],
        compiler_params=pltpu.CompilerParams(vmem_limit_bytes=48 << 20),
        cost_estimate=pl.CostEstimate(flops=4 * 768 * 256 * 2880, bytes_accessed=12_000_000, transcendentals=0),
        name="combine",
    )(y, rows, meta, sib_meta)


def ring(axis, shift, n):
    return functools.partial(lax.ppermute, axis_name=axis, perm=[(i, (i + shift) % n) for i in range(n)])


def gather_ring4(block, axis):
    half = block.shape[0] // 2
    below = ring(axis, 1, 4)(block)
    above = ring(axis, -1, 4)(block)
    far = jnp.concatenate([ring(axis, 1, 4)(below[:half]), ring(axis, -1, 4)(above[half:])], axis=0)
    return block, below, above, far


def projection(context, og_t):
    y, zl = lax.axis_index("y"), lax.axis_index("zl")
    x, core, zh = lax.axis_index("x"), lax.axis_index("core"), lax.axis_index("zh")
    other = ring("zl", 1, 2)(og_t)
    pair = jnp.stack([jnp.where(zl == 0, og_t, other), jnp.where(zl == 0, other, og_t)])
    ctx = context.reshape(4, 2, 128, 512)
    grad = None
    for at, block in zip((0, 3, 1, 2), gather_ring4(pair, "y")):
        own_ctx = lax.dynamic_index_in_dim(ctx, (y + at) % 4, 0, keepdims=False)
        term = lax.dot_general(block, own_ctx, (((0, 2), (0, 1)), ((), ())), preferred_element_type=F32)
        grad = term if grad is None else grad + term
    grad = grad.astype(BF)
    halves = grad.reshape(2, 1440, 512)
    mine = lax.dynamic_index_in_dim(halves, core, 0, keepdims=False)
    sent = lax.dynamic_index_in_dim(halves, 1 - core, 0, keepdims=False)
    part = mine.astype(F32) + ring("core", 1, 2)(sent).astype(F32)
    cols = part.reshape(1440, 4, 128).swapaxes(0, 1)

    def block_of(offset):
        return lax.dynamic_index_in_dim(cols, (x + offset) % 4, 0, keepdims=False)

    far = block_of(2).astype(BF)
    from_below = ring("x", 1, 4)(far[:720])
    from_above = ring("x", -1, 4)(far[720:])
    up, down = block_of(1), block_of(3)
    up = jnp.concatenate([up[:720] + from_below.astype(F32), up[720:]]).astype(BF)
    down = jnp.concatenate([down[:720], down[720:] + from_above.astype(F32)]).astype(BF)
    block = block_of(0) + ring("x", 1, 4)(up).astype(F32) + ring("x", -1, 4)(down).astype(F32)
    rows = block.reshape(2, 720, 128)
    kept = lax.dynamic_index_in_dim(rows, zh, 0, keepdims=False)
    gone = lax.dynamic_index_in_dim(rows, 1 - zh, 0, keepdims=False).astype(BF)
    total = (kept + ring("zh", 1, 2)(gone).astype(F32)).astype(BF)
    back = ring("zh", 1, 2)(total)
    block = jnp.concatenate([jnp.where(zh == 0, total, back), jnp.where(zh == 0, back, total)])
    ordered = jnp.stack(gather_ring4(block, "x"))
    at = jnp.array([0, 3, 1, 2])
    source = jnp.take(at.argsort(), (jnp.arange(4) - x) % 4)
    full = jnp.take(ordered, source, axis=0)
    full = full.swapaxes(0, 1).reshape(1440, 512)
    opposite = ring("core", 1, 2)(full)
    both = jnp.concatenate([jnp.where(core == 0, full, opposite), jnp.where(core == 0, opposite, full)])
    return both.astype(F32)


def local(tokens, expert_ids, gate_raw, overflow_shift, limits, gate_w, up_w, down_w, context, out_grad):
    tok = tokens.T
    meta = jnp.concatenate([expert_ids.T.astype(F32), overflow_shift.T.astype(F32), gate_raw.T, jnp.zeros((4, 128), F32)])
    swap = ring("core", 1, 2)
    sib_tok, sib_meta = swap(tok), swap(meta)
    lim = jnp.broadcast_to(limits.astype(F32)[:, None], (64, 128))
    core = lax.axis_index("core")
    send, rows = dispatch(tok, sib_tok, meta, sib_meta, lim, core[None])
    over = ("zl", "x", "zh", "y")
    got = lax.all_to_all(send.reshape(64, 24, 2880), over, split_axis=0, concat_axis=0, tiled=True)
    partial_out = ffn(got.reshape(1536, 2880), gate_w, up_w, down_w[0].T)
    back = lax.all_to_all(partial_out.reshape(64, 24, 2880), over, split_axis=0, concat_axis=0, tiled=True)
    own, sib = combine(back.reshape(2, 768, 2880), rows, meta, sib_meta)
    mixed = (own + swap(sib).astype(F32)).astype(BF)
    grad = projection(context, out_grad.T)
    return mixed.T, grad.T


def solution(mesh):
    fine = Mesh(mesh.devices.reshape(4, 2, 2, 4, 2), ("x", "zh", "core", "y", "zl"))
    every = ("x", "zh", "core", "y", "zl")
    two, three = P(every, None), P(every, None, None)
    in_specs = (two, two, two, two, P(), three, three, three, P(("x", "zh", "core"), ("y", "zl")), two)
    out_specs = (two, P(("y", "zl"), None))
    return jax.shard_map(local, mesh=fine, in_specs=in_specs, out_specs=out_specs, check_vma=False)
```

```python
import functools

import jax
import jax.numpy as jnp
from jax import lax
from jax.experimental import pallas as pl
from jax.experimental.pallas import tpu as pltpu
from jax.sharding import Mesh, PartitionSpec as P

CAP = 12
BF = jnp.bfloat16
F32 = jnp.float32
NT = (((1,), (1,)), ((), ()))


def place(ids, shifts, lim):
    label = lax.broadcasted_iota(jnp.int32, (64, 128), 0)
    earlier = (
        lax.broadcasted_iota(jnp.int32, (128, 128), 0)
        < lax.broadcasted_iota(jnp.int32, (128, 128), 1)
    ).astype(F32).astype(BF)
    rows = [ids[k : k + 1, :] for k in range(4)]
    hots = [(r == label).astype(F32) for r in rows]
    hot = hots[0] + hots[1] + hots[2] + hots[3]
    before = jnp.dot(hot.astype(BF), earlier, preferred_element_type=F32)
    spilled, seconds, second_hots, first_ranks = [], [], [], []
    for k in range(4):
        rank = jnp.sum(before * hots[k], axis=0, keepdims=True)
        limit = jnp.sum(lim * hots[k], axis=0, keepdims=True)
        spill = rank >= limit
        second = (rows[k] + shifts[k : k + 1, :]) & 63
        first_ranks.append(rank)
        spilled.append(spill)
        seconds.append(second)
        second_hots.append((second == label).astype(F32))
    spill_hots = [h * s.astype(F32) for h, s in zip(second_hots, spilled)]
    total = spill_hots[0] + spill_hots[1] + spill_hots[2] + spill_hots[3]
    run = jnp.dot(total.astype(BF), earlier, preferred_element_type=F32)
    out = []
    for k in range(4):
        rank = jnp.sum(run * second_hots[k], axis=0, keepdims=True)
        run = run + spill_hots[k]
        limit = jnp.sum(lim * second_hots[k], axis=0, keepdims=True)
        slot = jnp.where(spilled[k], limit + rank, first_ranks[k]).astype(jnp.int32)
        target = jnp.where(spilled[k], seconds[k], rows[k])
        out.append((target, slot, slot < CAP))
    return out


def place_kernel(tok_ref, ids_ref, shift_ref, raw_ref, lim_ref, out_ref):
    out_ref[:2880, :] = tok_ref[...]
    places = place(ids_ref[...], shift_ref[...], lim_ref[...])
    raw = raw_ref[...]
    share = raw / jnp.sum(raw, axis=0, keepdims=True)
    rows = [t.astype(F32) for t, _, _ in places]
    rows += [jnp.where(k, s, -1).astype(F32) for _, s, k in places]
    rows += [share, jnp.zeros((4, 128), F32)]
    out_ref[2880:, :] = jnp.concatenate(rows, axis=0).astype(BF)


def place_call(tok, ids, shifts, raw, lim):
    vm = pl.BlockSpec(memory_space=pltpu.VMEM)
    return pl.pallas_call(
        place_kernel,
        in_specs=[vm] * 5,
        out_specs=vm,
        out_shape=jax.ShapeDtypeStruct((2896, 128), BF),
        compiler_params=pltpu.CompilerParams(vmem_limit_bytes=16 << 20),
        cost_estimate=pl.CostEstimate(flops=1 << 22, bytes_accessed=1_500_000, transcendentals=0),
        name="place",
    )(tok, ids, shifts, raw, lim)


def row_hot(tail, core, y, side):
    tail = tail.astype(F32)
    at = lax.broadcasted_iota(jnp.int32, (192, 128), 0)
    hot = None
    for k in range(4):
        target = tail[k : k + 1].astype(jnp.int32)
        slot = tail[4 + k : 5 + k].astype(jnp.int32)
        mine = (slot >= 0) & (((target >> 2) & 1) == core) & ((target & 3) == y)
        one = jnp.where(mine, (target >> 3) * 24 + side * CAP + slot, -1) == at
        hot = one if hot is None else hot | one
    return hot.astype(F32).astype(BF)


def picked_rows(own_ref, sib_ref, core, y):
    hot = jnp.concatenate(
        [row_hot(own_ref[2880:, :], core, y, 0), row_hot(sib_ref[2880:, :], core, y, 1)], axis=1
    )
    both = jnp.concatenate([own_ref[:2880, :], sib_ref[:2880, :]], axis=1)
    return lax.dot_general(hot, both, NT, preferred_element_type=F32)


def near_kernel(at_ref, own_ref, sib_ref, out_ref):
    got = picked_rows(own_ref, sib_ref, at_ref[0], at_ref[1]).astype(BF)
    out_ref[0] = got
    out_ref[1] = got


def near_rows(at, own, sib):
    vm = pl.BlockSpec(memory_space=pltpu.VMEM)
    return pl.pallas_call(
        near_kernel,
        in_specs=[pl.BlockSpec(memory_space=pltpu.SMEM), vm, vm],
        out_specs=vm,
        out_shape=jax.ShapeDtypeStruct((2, 192, 2880), BF),
        compiler_params=pltpu.CompilerParams(vmem_limit_bytes=24 << 20),
        cost_estimate=pl.CostEstimate(flops=2 * 192 * 256 * 2880, bytes_accessed=3_700_000, transcendentals=0),
        name="near_rows",
    )(at, own, sib)


def far_kernel(at_ref, *refs):
    out_ref = refs[6]
    for o in range(3):

        @pl.when(pl.program_id(0) == o)
        def _(o=o):
            got = picked_rows(refs[2 * o], refs[2 * o + 1], at_ref[0], at_ref[1])
            got = got.reshape(8, 24, 2880).astype(BF)
            out_ref[0, :, 0] = got
            out_ref[1, :, 0] = got


def far_rows(at, blocks):
    vm = pl.BlockSpec(memory_space=pltpu.VMEM)
    return pl.pallas_call(
        far_kernel,
        grid=(3,),
        in_specs=[pl.BlockSpec(memory_space=pltpu.SMEM)] + [vm] * 6,
        out_specs=pl.BlockSpec((2, 8, 1, 24, 2880), lambda i: (0, 0, i, 0, 0)),
        out_shape=jax.ShapeDtypeStruct((2, 8, 3, 24, 2880), BF),
        compiler_params=pltpu.CompilerParams(vmem_limit_bytes=48 << 20),
        cost_estimate=pl.CostEstimate(flops=6 * 192 * 256 * 2880, bytes_accessed=11_000_000, transcendentals=0),
        name="far_rows",
    )(at, *blocks)


def ffn_kernel(near, at_ref, x_ref, g_ref, u_ref, d_ref, *refs):
    out_ref = refs[-1]
    x = x_ref[...] if near else x_ref[:, 0].reshape(384, 2880)
    gating = jnp.dot(x, g_ref[...], preferred_element_type=F32)
    upward = jnp.dot(x, u_ref[...], preferred_element_type=F32)
    active = ((upward + 1.0) * gating * jax.nn.sigmoid(1.702 * gating)).astype(BF)
    got = lax.dot_general(active, d_ref[...], NT, preferred_element_type=F32)
    out_ref[:, 0] = got.reshape(16, 24, 2880).astype(BF)


def ffn_part(at, o, x, g, u, d_t, into=None):
    vm = pl.BlockSpec(memory_space=pltpu.VMEM)
    if o == 0:
        x_spec = pl.BlockSpec((384, 2880), lambda i, at: (0, 0))
    else:
        x_spec = pl.BlockSpec((16, 1, 24, 2880), lambda i, at: (0, o - 1, 0, 0))
    args = (at, x, g, u, d_t) + (() if into is None else (into,))
    return pl.pallas_call(
        functools.partial(ffn_kernel, o == 0),
        grid_spec=pltpu.PrefetchScalarGridSpec(
            num_scalar_prefetch=1,
            grid=(1,),
            in_specs=[x_spec, vm, vm, vm] + ([] if into is None else [pl.BlockSpec(memory_space=pltpu.HBM)]),
            out_specs=pl.BlockSpec((16, 1, 24, 2880), lambda i, at: (0, (at[1] + o) & 3, 0, 0)),
        ),
        out_shape=pltpu.HBM((16, 4, 24, 2880), BF),
        input_output_aliases={} if into is None else {5: 0},
        compiler_params=pltpu.CompilerParams(vmem_limit_bytes=30 << 20),
        cost_estimate=pl.CostEstimate(
            flops=6 * 384 * 2880 * 768, bytes_accessed=18_000_000, transcendentals=384 * 768
        ),
        name="ffn_part",
    )(*args)


def first_kernel(at_ref, x_ref, g_hbm, u_hbm, d_hbm, out_ref, g_ref, u_ref, d_ref, sems):
    copies = [
        pltpu.make_async_copy(g_hbm.at[0], g_ref, sems.at[0]),
        pltpu.make_async_copy(u_hbm.at[0], u_ref, sems.at[1]),
        pltpu.make_async_copy(d_hbm, d_ref, sems.at[2]),
    ]
    for c in copies:
        c.start()
    x = x_ref[:, 0].reshape(384, 2880)
    copies[0].wait()
    gating = jnp.dot(x, g_ref[...], preferred_element_type=F32)
    copies[1].wait()
    upward = jnp.dot(x, u_ref[...], preferred_element_type=F32)
    active = ((upward + 1.0) * gating * jax.nn.sigmoid(1.702 * gating)).astype(BF)
    copies[2].wait()
    got = lax.dot_general(active, d_ref[...], NT, preferred_element_type=F32)
    out_ref[:, 0] = got.reshape(16, 24, 2880).astype(BF)


def ffn_first(at, x, g, u, d_t):
    hbm = pl.BlockSpec(memory_space=pltpu.HBM)
    return pl.pallas_call(
        first_kernel,
        grid_spec=pltpu.PrefetchScalarGridSpec(
            num_scalar_prefetch=1,
            grid=(1,),
            in_specs=[pl.BlockSpec((16, 1, 24, 2880), lambda i, at: (0, 0, 0, 0)), hbm, hbm, hbm],
            out_specs=[pl.BlockSpec((16, 1, 24, 2880), lambda i, at: (0, (at[1] + 1) & 3, 0, 0))]
            + [pl.BlockSpec(memory_space=pltpu.VMEM)] * 3,
            scratch_shapes=[pltpu.SemaphoreType.DMA((3,))],
        ),
        out_shape=[pltpu.HBM((16, 4, 24, 2880), BF)] + [pltpu.VMEM((2880, 768), BF)] * 3,
        compiler_params=pltpu.CompilerParams(vmem_limit_bytes=47 << 20),
        cost_estimate=pl.CostEstimate(
            flops=6 * 384 * 2880 * 768, bytes_accessed=18_000_000, transcendentals=384 * 768
        ),
        name="ffn_first",
    )(at, x, g, u, d_t)


def combine_kernel(at_ref, y_ref, own_tail_ref, sib_tail_ref, own_ref, sib_ref, w_ref, acc_ref):
    step = pl.program_id(0)

    @pl.when(step == 0)
    def _():
        core = at_ref[0]
        slot_of = lax.broadcasted_iota(jnp.int32, (768, 128), 0)
        for side, ref in enumerate((own_tail_ref, sib_tail_ref)):
            tail = ref[...].astype(F32)
            w = jnp.zeros((768, 128), F32)
            for k in range(4):
                target = tail[k : k + 1].astype(jnp.int32)
                slot = tail[4 + k : 5 + k].astype(jnp.int32)
                mine = (slot >= 0) & (((target >> 2) & 1) == core)
                row = jnp.where(mine, ((target >> 3) * 4 + (target & 3)) * 24 + side * CAP + slot, -1)
                w = w + jnp.where(row == slot_of, tail[8 + k : 9 + k], 0.0)
            wt = w.T.astype(BF)
            for b in range(4):
                w_ref[b, 128 * side : 128 * side + 128, :] = wt[:, 192 * b : 192 * b + 192]
        acc_ref[...] = jnp.zeros_like(acc_ref)

    w = w_ref[step]
    acc_ref[...] += jnp.dot(w, y_ref[0], preferred_element_type=F32) + jnp.dot(
        w, y_ref[1], preferred_element_type=F32
    )

    @pl.when(step == 3)
    def _():
        own_ref[...] = acc_ref[:128, :].T
        sib_ref[...] = acc_ref[128:, :].T.astype(BF)


def combine(at, y, own_tail, sib_tail):
    vm = pl.BlockSpec(memory_space=pltpu.VMEM)
    return pl.pallas_call(
        combine_kernel,
        grid=(4,),
        in_specs=[
            pl.BlockSpec(memory_space=pltpu.SMEM),
            pl.BlockSpec((2, 192, 2880), lambda i: (0, i, 0)),
            vm,
            vm,
        ],
        out_specs=[pl.BlockSpec((2880, 128), lambda i: (0, 0))] * 2,
        out_shape=[jax.ShapeDtypeStruct((2880, 128), F32), jax.ShapeDtypeStruct((2880, 128), BF)],
        scratch_shapes=[pltpu.VMEM((4, 256, 192), BF), pltpu.VMEM((256, 2880), F32)],
        compiler_params=pltpu.CompilerParams(vmem_limit_bytes=48 << 20),
        cost_estimate=pl.CostEstimate(flops=4 * 768 * 256 * 2880, bytes_accessed=12_000_000, transcendentals=0),
        name="combine",
    )(at, y, own_tail, sib_tail)


def grad_kernel(at_ref, p0_ref, p1_ref, p2_ref, p3_ref, ctx_ref, out_ref):
    y, zl, x = at_ref[1], at_ref[2], at_ref[3]
    total = None
    for o, ref in enumerate((p0_ref, p1_ref, p2_ref, p3_ref)):
        base = ((y + o) & 3) * 256
        same = ctx_ref[pl.ds(pl.multiple_of(base + zl * 128, 128), 128), :]
        other = ctx_ref[pl.ds(pl.multiple_of(base + (1 - zl) * 128, 128), 128), :]
        left = jnp.concatenate([ref[0], ref[1]], axis=1)
        term = jnp.dot(left, jnp.concatenate([same, other], axis=0), preferred_element_type=F32)
        total = term if total is None else total + term
    for j in range(4):
        out_ref[0, pl.ds((j - x) & 3, 1)] = total[None, :, 128 * j : 128 * j + 128].astype(BF)


def local_grad(at, pairs, context):
    return pl.pallas_call(
        grad_kernel,
        grid_spec=pltpu.PrefetchScalarGridSpec(
            num_scalar_prefetch=1,
            grid=(4,),
            in_specs=[pl.BlockSpec((2, 720, 128), lambda i, at: (0, i, 0))] * 4
            + [pl.BlockSpec(memory_space=pltpu.VMEM)],
            out_specs=pl.BlockSpec((1, 4, 720, 128), lambda i, at: ((i >> 1) ^ at[0], 0, i & 1, 0)),
        ),
        out_shape=jax.ShapeDtypeStruct((2, 4, 1440, 128), BF),
        compiler_params=pltpu.CompilerParams(vmem_limit_bytes=24 << 20),
        cost_estimate=pl.CostEstimate(flops=2 * 1024 * 512 * 2880, bytes_accessed=10_000_000, transcendentals=0),
        name="local_grad",
    )(at, *pairs, context)


def spread_kernel(at_ref, own_ref, sib_ref, out_ref):
    core = at_ref[0]
    out_ref[pl.ds(core, 1)] = own_ref[...].astype(F32)
    out_ref[pl.ds(1 - core, 1)] = sib_ref[...].astype(F32)


def spread(at, own, sib):
    block = pl.BlockSpec((1, 1440, 128), lambda i, at: (i, 0, 0))
    return pl.pallas_call(
        spread_kernel,
        grid_spec=pltpu.PrefetchScalarGridSpec(
            num_scalar_prefetch=1,
            grid=(4,),
            in_specs=[block, block],
            out_specs=pl.BlockSpec((2, 1440, 128), lambda i, at: (0, 0, (at[3] + i) & 3)),
        ),
        out_shape=jax.ShapeDtypeStruct((2, 1440, 512), F32),
        compiler_params=pltpu.CompilerParams(vmem_limit_bytes=16 << 20),
        cost_estimate=pl.CostEstimate(flops=0, bytes_accessed=9_000_000, transcendentals=0),
        name="spread",
    )(at, own, sib)


def shift(axis, by, n):
    return functools.partial(lax.ppermute, axis_name=axis, perm=[(i, (i + by) % n) for i in range(n)])


def from_others(block, axis):
    return [shift(axis, -o, 4)(block) for o in (1, 2, 3)]


def after(value, *others):
    return lax.optimization_barrier((value,) + others)[0]


def local(tokens, expert_ids, gate_raw, overflow_shift, limits, gate_w, up_w, down_w, context, out_grad):
    at = jnp.stack([lax.axis_index(a) for a in ("core", "y", "zl", "x", "zh")]).astype(jnp.int32)
    zh = lax.axis_index("zh")
    core_swap, zl_swap, zh_swap = shift("core", 1, 2), shift("zl", 1, 2), shift("zh", 1, 2)
    over = ("zl", "x", "zh")

    lim = jnp.broadcast_to(limits.astype(F32)[:, None], (64, 128))
    mine = place_call(tokens.T, expert_ids.T, overflow_shift.T, gate_raw.T, lim)
    og = out_grad.T
    og_other = zl_swap(og)
    sibling = core_swap(mine)
    others = from_others(mine, "y")
    near = near_rows(at, mine, sibling).reshape(16, 24, 2880)
    near = lax.all_to_all(near, over, split_axis=0, concat_axis=0, tiled=True)
    blocks = []
    for block in others:
        blocks += [block, core_swap(block)]
    pair = jnp.stack([og, og_other])
    far = after(far_rows(at, blocks), pair, near).reshape(16, 72, 2880)
    far = lax.all_to_all(far, over, split_axis=0, concat_axis=0, tiled=True)

    pairs = [pair] + from_others(pair, "y")
    grads = local_grad(at, pairs, context)
    part = grads[0].astype(F32) + core_swap(grads[1]).astype(F32)
    total = part[0]
    for o in (1, 2, 3):
        total = total + shift("x", o, 4)(part[o].astype(BF)).astype(F32)
    far = far.reshape(16, 3, 24, 2880)
    rows = total.reshape(2, 720, 128)
    kept = lax.dynamic_index_in_dim(rows, zh, 0, keepdims=False)
    gone = lax.dynamic_index_in_dim(rows, 1 - zh, 0, keepdims=False).astype(BF)
    came = zh_swap(gone)
    out, *weights = ffn_first(at, after(far, gone), gate_w, up_w, down_w[0].T)
    total = (kept + after(came, out).astype(F32)).astype(BF)
    back = zh_swap(total)
    out = ffn_part(at, 2, far, *weights, after(out, total))
    back = after(back, out)
    block = jnp.concatenate([jnp.where(zh == 0, total, back), jnp.where(zh == 0, back, total)])
    blocks = from_others(block, "x")
    out = ffn_part(at, 3, far, *weights, after(out, block))
    out = ffn_part(at, 0, near.reshape(384, 2880), *weights, out)
    out = after(out, *blocks)
    full = jnp.stack([block] + blocks)
    grad = spread(at, full, core_swap(full)).reshape(2880, 512)

    out = lax.all_to_all(out.reshape(64, 24, 2880), over + ("y",), split_axis=0, concat_axis=0, tiled=True)
    own, sib = combine(at, out.reshape(2, 768, 2880), mine[2880:], sibling[2880:])
    mixed = (own + core_swap(sib).astype(F32)).astype(BF)
    return mixed.T, grad.T


def solution(mesh):
    fine = Mesh(mesh.devices.reshape(4, 2, 2, 4, 2), ("x", "zh", "core", "y", "zl"))
    every = ("x", "zh", "core", "y", "zl")
    two, three = P(every, None), P(every, None, None)
    in_specs = (two, two, two, two, P(), three, three, three, P(("x", "zh", "core"), ("y", "zl")), two)
    out_specs = (two, P(("y", "zl"), None))
    return jax.shard_map(local, mesh=fine, in_specs=in_specs, out_specs=out_specs, check_vma=False)
```

```python
import functools

import jax
import jax.numpy as jnp
from jax import lax
from jax.experimental import pallas as pl
from jax.experimental.pallas import tpu as pltpu
from jax.sharding import Mesh, PartitionSpec as P

CAP = 12
BF = jnp.bfloat16
F32 = jnp.float32
NT = (((1,), (1,)), ((), ()))


def place(ids, shifts, lim):
    label = lax.broadcasted_iota(jnp.int32, (64, 128), 0)
    earlier = (
        lax.broadcasted_iota(jnp.int32, (128, 128), 0)
        < lax.broadcasted_iota(jnp.int32, (128, 128), 1)
    ).astype(F32).astype(BF)
    rows = [ids[k : k + 1, :] for k in range(4)]
    hots = [(r == label).astype(F32) for r in rows]
    hot = hots[0] + hots[1] + hots[2] + hots[3]
    before = jnp.dot(hot.astype(BF), earlier, preferred_element_type=F32)
    spilled, seconds, second_hots, first_ranks = [], [], [], []
    for k in range(4):
        rank = jnp.sum(before * hots[k], axis=0, keepdims=True)
        limit = jnp.sum(lim * hots[k], axis=0, keepdims=True)
        spill = rank >= limit
        second = (rows[k] + shifts[k : k + 1, :]) & 63
        first_ranks.append(rank)
        spilled.append(spill)
        seconds.append(second)
        second_hots.append((second == label).astype(F32))
    spill_hots = [h * s.astype(F32) for h, s in zip(second_hots, spilled)]
    total = spill_hots[0] + spill_hots[1] + spill_hots[2] + spill_hots[3]
    run = jnp.dot(total.astype(BF), earlier, preferred_element_type=F32)
    out = []
    for k in range(4):
        rank = jnp.sum(run * second_hots[k], axis=0, keepdims=True)
        run = run + spill_hots[k]
        limit = jnp.sum(lim * second_hots[k], axis=0, keepdims=True)
        slot = jnp.where(spilled[k], limit + rank, first_ranks[k]).astype(jnp.int32)
        target = jnp.where(spilled[k], seconds[k], rows[k])
        out.append((target, slot, slot < CAP))
    return out


def place_kernel(tok_ref, ids_ref, shift_ref, raw_ref, lim_ref, out_ref):
    out_ref[:2880, :] = tok_ref[...]
    places = place(ids_ref[...], shift_ref[...], lim_ref[...])
    raw = raw_ref[...]
    share = raw / jnp.sum(raw, axis=0, keepdims=True)
    rows = [t.astype(F32) for t, _, _ in places]
    rows += [jnp.where(k, s, -1).astype(F32) for _, s, k in places]
    rows += [share, jnp.zeros((4, 128), F32)]
    out_ref[2880:, :] = jnp.concatenate(rows, axis=0).astype(BF)


def place_call(tok, ids, shifts, raw, lim):
    vm = pl.BlockSpec(memory_space=pltpu.VMEM)
    return pl.pallas_call(
        place_kernel,
        in_specs=[vm] * 5,
        out_specs=vm,
        out_shape=jax.ShapeDtypeStruct((2896, 128), BF),
        compiler_params=pltpu.CompilerParams(vmem_limit_bytes=16 << 20),
        cost_estimate=pl.CostEstimate(flops=1 << 22, bytes_accessed=1_500_000, transcendentals=0),
        name="place",
    )(tok, ids, shifts, raw, lim)


def row_hot(tail, core, y, side):
    tail = tail.astype(F32)
    at = lax.broadcasted_iota(jnp.int32, (192, 128), 0)
    hot = None
    for k in range(4):
        target = tail[k : k + 1].astype(jnp.int32)
        slot = tail[4 + k : 5 + k].astype(jnp.int32)
        mine = (slot >= 0) & (((target >> 2) & 1) == core) & ((target & 3) == y)
        one = jnp.where(mine, (target >> 3) * 24 + side * CAP + slot, -1) == at
        hot = one if hot is None else hot | one
    return hot.astype(F32).astype(BF)


def picked_rows(own_ref, sib_ref, core, y):
    hot = jnp.concatenate(
        [row_hot(own_ref[2880:, :], core, y, 0), row_hot(sib_ref[2880:, :], core, y, 1)], axis=1
    )
    both = jnp.concatenate([own_ref[:2880, :], sib_ref[:2880, :]], axis=1)
    return lax.dot_general(hot, both, NT, preferred_element_type=F32)


def near_kernel(at_ref, own_ref, sib_ref, out_ref):
    got = picked_rows(own_ref, sib_ref, at_ref[0], at_ref[1]).astype(BF)
    out_ref[0] = got
    out_ref[1] = got


def near_rows(at, own, sib):
    vm = pl.BlockSpec(memory_space=pltpu.VMEM)
    return pl.pallas_call(
        near_kernel,
        in_specs=[pl.BlockSpec(memory_space=pltpu.SMEM), vm, vm],
        out_specs=vm,
        out_shape=jax.ShapeDtypeStruct((2, 192, 2880), BF),
        compiler_params=pltpu.CompilerParams(vmem_limit_bytes=24 << 20),
        cost_estimate=pl.CostEstimate(flops=2 * 192 * 256 * 2880, bytes_accessed=3_700_000, transcendentals=0),
        name="near_rows",
    )(at, own, sib)


def far_kernel(at_ref, *refs):
    out_ref = refs[6]
    for o in range(3):

        @pl.when(pl.program_id(0) == o)
        def _(o=o):
            got = picked_rows(refs[2 * o], refs[2 * o + 1], at_ref[0], at_ref[1])
            got = got.reshape(8, 24, 2880).astype(BF)
            out_ref[0, :, 0] = got
            out_ref[1, :, 0] = got


def far_rows(at, blocks):
    vm = pl.BlockSpec(memory_space=pltpu.VMEM)
    return pl.pallas_call(
        far_kernel,
        grid=(3,),
        in_specs=[pl.BlockSpec(memory_space=pltpu.SMEM)] + [vm] * 6,
        out_specs=pl.BlockSpec((2, 8, 1, 24, 2880), lambda i: (0, 0, i, 0, 0)),
        out_shape=jax.ShapeDtypeStruct((2, 8, 3, 24, 2880), BF),
        compiler_params=pltpu.CompilerParams(vmem_limit_bytes=48 << 20),
        cost_estimate=pl.CostEstimate(flops=6 * 192 * 256 * 2880, bytes_accessed=11_000_000, transcendentals=0),
        name="far_rows",
    )(at, *blocks)


def ffn_rows(x, g_ref, u_ref, d_ref, copies=(None,) * 3):
    def ready(i):
        if copies[i] is not None:
            copies[i].wait()

    ready(0)
    gating = jnp.dot(x, g_ref[...], preferred_element_type=F32)
    ready(1)
    upward = jnp.dot(x, u_ref[...], preferred_element_type=F32)
    active = ((upward + 1.0) * gating * jax.nn.sigmoid(1.702 * gating)).astype(BF)
    ready(2)
    return lax.dot_general(active, d_ref[...], NT, preferred_element_type=F32)


def started(g_hbm, u_hbm, d_hbm, g_ref, u_ref, d_ref, sems):
    copies = [
        pltpu.make_async_copy(g_hbm.at[0], g_ref, sems.at[0]),
        pltpu.make_async_copy(u_hbm.at[0], u_ref, sems.at[1]),
        pltpu.make_async_copy(d_hbm, d_ref, sems.at[2]),
    ]
    for c in copies:
        c.start()
    return copies


def near_ffn_kernel(at_ref, x_ref, g_hbm, u_hbm, d_hbm, out_ref, g_ref, u_ref, d_ref, sems):
    copies = started(g_hbm, u_hbm, d_hbm, g_ref, u_ref, d_ref, sems)
    got = ffn_rows(x_ref[...], g_ref, u_ref, d_ref, copies)
    out_ref[:, 0] = got.reshape(16, 24, 2880).astype(BF)


def first_kernel(at_ref, x_ref, g_hbm, u_hbm, d_hbm, into_ref, out_ref, g_ref, u_ref, d_ref, sems):
    copies = started(g_hbm, u_hbm, d_hbm, g_ref, u_ref, d_ref, sems)
    got = ffn_rows(x_ref[:, 0].reshape(384, 2880), g_ref, u_ref, d_ref, copies)
    out_ref[:, 0] = got.reshape(16, 24, 2880).astype(BF)


def part_kernel(at_ref, x_ref, g_ref, u_ref, d_ref, into_ref, out_ref):
    got = ffn_rows(x_ref[:, 0].reshape(384, 2880), g_ref, u_ref, d_ref)
    out_ref[:, 0] = got.reshape(16, 24, 2880).astype(BF)


def ffn_part(at, o, x, g, u, d_t, into=None):
    hbm, vm = pl.BlockSpec(memory_space=pltpu.HBM), pl.BlockSpec(memory_space=pltpu.VMEM)
    kernel = (near_ffn_kernel, first_kernel, part_kernel, part_kernel)[o]
    held = [pltpu.VMEM((2880, 768), BF)] * 3
    sems = [pltpu.SemaphoreType.DMA((3,))]
    if o == 0:
        x_spec = pl.BlockSpec((384, 2880), lambda i, at: (0, 0))
    else:
        x_spec = pl.BlockSpec((16, 1, 24, 2880), lambda i, at: (0, o - 1, 0, 0))
    return pl.pallas_call(
        kernel,
        grid_spec=pltpu.PrefetchScalarGridSpec(
            num_scalar_prefetch=1,
            grid=(1,),
            in_specs=[x_spec] + [vm if o > 1 else hbm] * 3 + [hbm] * (o > 0),
            out_specs=[pl.BlockSpec((16, 1, 24, 2880), lambda i, at: (0, (at[1] + o) & 3, 0, 0))]
            + [vm] * 3 * (o == 1),
            scratch_shapes=(held + sems, sems, [], [])[o],
        ),
        out_shape=[pltpu.HBM((16, 4, 24, 2880), BF)] + held * (o == 1),
        input_output_aliases={5: 0} if o else {},
        compiler_params=pltpu.CompilerParams(vmem_limit_bytes=(60, 47, 30, 30)[o] << 20),
        cost_estimate=pl.CostEstimate(
            flops=6 * 384 * 2880 * 768, bytes_accessed=18_000_000, transcendentals=384 * 768
        ),
        name="ffn_part%d" % o,
    )(at, x, g, u, d_t, *([into] if o else []))


def combine_kernel(at_ref, y_ref, own_tail_ref, sib_tail_ref, ahead_ref, own_ref, sib_ref, w_ref, acc_ref):
    step = pl.program_id(0)

    @pl.when(step == 0)
    def _():
        core = at_ref[0]
        slot_of = lax.broadcasted_iota(jnp.int32, (768, 128), 0)
        for side, ref in enumerate((own_tail_ref, sib_tail_ref)):
            tail = ref[...].astype(F32)
            w = jnp.zeros((768, 128), F32)
            for k in range(4):
                target = tail[k : k + 1].astype(jnp.int32)
                slot = tail[4 + k : 5 + k].astype(jnp.int32)
                mine = (slot >= 0) & (((target >> 2) & 1) == core)
                row = jnp.where(mine, ((target >> 3) * 4 + (target & 3)) * 24 + side * CAP + slot, -1)
                w = w + jnp.where(row == slot_of, tail[8 + k : 9 + k], 0.0)
            wt = w.T.astype(BF)
            for b in range(4):
                w_ref[b, 128 * side : 128 * side + 128, :] = wt[:, 192 * b : 192 * b + 192]
        acc_ref[...] = jnp.zeros_like(acc_ref)

    w = w_ref[step]
    acc_ref[...] += jnp.dot(w, y_ref[0], preferred_element_type=F32) + jnp.dot(
        w, y_ref[1], preferred_element_type=F32
    )

    @pl.when(step == 3)
    def _():
        own_ref[...] = acc_ref[:128, :].T
        sib_ref[...] = acc_ref[128:, :].T.astype(BF)


def combine(at, y, own_tail, sib_tail, ahead):
    vm = pl.BlockSpec(memory_space=pltpu.VMEM)
    return pl.pallas_call(
        combine_kernel,
        grid=(4,),
        in_specs=[
            pl.BlockSpec(memory_space=pltpu.SMEM),
            pl.BlockSpec((2, 192, 2880), lambda i: (0, i, 0)),
            vm,
            vm,
            pl.BlockSpec(memory_space=pl.ANY),
        ],
        out_specs=[pl.BlockSpec((2880, 128), lambda i: (0, 0))] * 2,
        out_shape=[jax.ShapeDtypeStruct((2880, 128), F32), jax.ShapeDtypeStruct((2880, 128), BF)],
        scratch_shapes=[pltpu.VMEM((4, 256, 192), BF), pltpu.VMEM((256, 2880), F32)],
        compiler_params=pltpu.CompilerParams(vmem_limit_bytes=48 << 20),
        cost_estimate=pl.CostEstimate(flops=4 * 768 * 256 * 2880, bytes_accessed=12_000_000, transcendentals=0),
        name="combine",
    )(at, y, own_tail, sib_tail, ahead)


def grad_kernel(at_ref, p0_ref, p1_ref, p2_ref, p3_ref, ctx_ref, out_ref):
    y, zl, x = at_ref[1], at_ref[2], at_ref[3]
    total = None
    for o, ref in enumerate((p0_ref, p1_ref, p2_ref, p3_ref)):
        base = ((y + o) & 3) * 256
        same = ctx_ref[pl.ds(pl.multiple_of(base + zl * 128, 128), 128), :]
        other = ctx_ref[pl.ds(pl.multiple_of(base + (1 - zl) * 128, 128), 128), :]
        left = jnp.concatenate([ref[0], ref[1]], axis=1)
        term = jnp.dot(left, jnp.concatenate([same, other], axis=0), preferred_element_type=F32)
        total = term if total is None else total + term
    for j in range(4):
        out_ref[0, pl.ds((j - x) & 3, 1)] = total[None, :, 128 * j : 128 * j + 128].astype(BF)


def local_grad(at, pairs, context):
    return pl.pallas_call(
        grad_kernel,
        grid_spec=pltpu.PrefetchScalarGridSpec(
            num_scalar_prefetch=1,
            grid=(4,),
            in_specs=[pl.BlockSpec((2, 720, 128), lambda i, at: (0, i, 0))] * 4
            + [pl.BlockSpec(memory_space=pltpu.VMEM)],
            out_specs=pl.BlockSpec((1, 4, 720, 128), lambda i, at: ((i >> 1) ^ at[0], 0, i & 1, 0)),
        ),
        out_shape=jax.ShapeDtypeStruct((2, 4, 1440, 128), BF),
        compiler_params=pltpu.CompilerParams(vmem_limit_bytes=24 << 20),
        cost_estimate=pl.CostEstimate(flops=2 * 1024 * 512 * 2880, bytes_accessed=10_000_000, transcendentals=0),
        name="local_grad",
    )(at, *pairs, context)


def spread_kernel(at_ref, own_ref, sib_ref, out_ref):
    core = at_ref[0]
    out_ref[pl.ds(core, 1)] = own_ref[...].astype(F32)
    out_ref[pl.ds(1 - core, 1)] = sib_ref[...].astype(F32)


def spread(at, own, sib):
    block = pl.BlockSpec((1, 1440, 128), lambda i, at: (i, 0, 0))
    return pl.pallas_call(
        spread_kernel,
        grid_spec=pltpu.PrefetchScalarGridSpec(
            num_scalar_prefetch=1,
            grid=(4,),
            in_specs=[block, block],
            out_specs=pl.BlockSpec((2, 1440, 128), lambda i, at: (0, 0, (at[3] + i) & 3)),
        ),
        out_shape=jax.ShapeDtypeStruct((2, 1440, 512), F32),
        compiler_params=pltpu.CompilerParams(vmem_limit_bytes=16 << 20),
        cost_estimate=pl.CostEstimate(flops=0, bytes_accessed=9_000_000, transcendentals=0),
        name="spread",
    )(at, own, sib)


def shift(axis, by, n):
    return functools.partial(lax.ppermute, axis_name=axis, perm=[(i, (i + by) % n) for i in range(n)])


def from_others(block, axis):
    return [shift(axis, -o, 4)(block) for o in (1, 2, 3)]


def after(value, *others):
    return lax.optimization_barrier((value,) + others)[0]


def local(tokens, expert_ids, gate_raw, overflow_shift, limits, gate_w, up_w, down_w, context, out_grad):
    at = jnp.stack([lax.axis_index(a) for a in ("core", "y", "zl", "x", "zh")]).astype(jnp.int32)
    zh = lax.axis_index("zh")
    core_swap, zl_swap, zh_swap = shift("core", 1, 2), shift("zl", 1, 2), shift("zh", 1, 2)
    over = ("zl", "x", "zh")

    lim = jnp.broadcast_to(limits.astype(F32)[:, None], (64, 128))
    mine = place_call(tokens.T, expert_ids.T, overflow_shift.T, gate_raw.T, lim)
    og = out_grad.T
    og_other = zl_swap(og)
    sibling = core_swap(mine)
    others = from_others(mine, "y")
    near = after(near_rows(at, mine, sibling), og_other, others[0], others[2]).reshape(16, 24, 2880)
    near = lax.all_to_all(near, over, split_axis=0, concat_axis=0, tiled=True)
    blocks = []
    for block in others:
        blocks += [block, core_swap(block)]
    pair = jnp.stack([og, og_other])
    far = after(far_rows(at, blocks), pair, near).reshape(16, 72, 2880)
    far = lax.all_to_all(far, over, split_axis=0, concat_axis=0, tiled=True)
    far = far.reshape(16, 3, 24, 2880)

    hbm_weights = gate_w, up_w, down_w[0].T
    (out,) = ffn_part(at, 0, near.reshape(384, 2880), *hbm_weights)
    pairs = [after(pair, out)] + from_others(pair, "y")
    grads = local_grad(at, pairs, context)
    part = grads[0].astype(F32) + core_swap(grads[1]).astype(F32)
    terms = [shift("x", o, 4)(part[o].astype(BF)) for o in (1, 2, 3)]
    out, *weights = ffn_part(at, 1, far, *hbm_weights, out)
    terms = lax.optimization_barrier((*terms, out))[:3]
    total = part[0] + terms[0].astype(F32) + terms[1].astype(F32) + terms[2].astype(F32)
    rows = total.reshape(2, 720, 128)
    kept = lax.dynamic_index_in_dim(rows, zh, 0, keepdims=False)
    gone = lax.dynamic_index_in_dim(rows, 1 - zh, 0, keepdims=False).astype(BF)
    came = zh_swap(gone)
    (out,) = ffn_part(at, 2, far, *weights, after(out, gone))
    total = (kept + after(came, out).astype(F32)).astype(BF)
    back = zh_swap(total)
    (out,) = ffn_part(at, 3, far, *weights, after(out, total))
    back = after(back, out)
    block = jnp.concatenate([jnp.where(zh == 0, total, back), jnp.where(zh == 0, back, total)])
    full = jnp.stack([block] + from_others(block, "x"))
    grad = spread(at, full, core_swap(full)).reshape(2880, 512)

    out = after(out, block).reshape(64, 24, 2880)
    out = lax.all_to_all(out, over + ("y",), split_axis=0, concat_axis=0, tiled=True)
    own, sib = combine(at, out.reshape(2, 768, 2880), mine[2880:], sibling[2880:], grad)
    mixed = (own + core_swap(sib).astype(F32)).astype(BF)
    return mixed.T, grad.T


def solution(mesh):
    fine = Mesh(mesh.devices.reshape(4, 2, 2, 4, 2), ("x", "zh", "core", "y", "zl"))
    every = ("x", "zh", "core", "y", "zl")
    two, three = P(every, None), P(every, None, None)
    in_specs = (two, two, two, two, P(), three, three, three, P(("x", "zh", "core"), ("y", "zl")), two)
    out_specs = (two, P(("y", "zl"), None))
    return jax.shard_map(local, mesh=fine, in_specs=in_specs, out_specs=out_specs, check_vma=False)
```

```python
import functools

import jax
import jax.numpy as jnp
from jax import lax
from jax.experimental import pallas as pl
from jax.experimental.pallas import tpu as pltpu
from jax.sharding import Mesh, PartitionSpec as P

CAP = 12
BF = jnp.bfloat16
F32 = jnp.float32
NT = (((1,), (1,)), ((), ()))


def place(ids, shifts, lim):
    label = lax.broadcasted_iota(jnp.int32, (64, 128), 0)
    earlier = (
        lax.broadcasted_iota(jnp.int32, (128, 128), 0)
        < lax.broadcasted_iota(jnp.int32, (128, 128), 1)
    ).astype(F32).astype(BF)
    rows = [ids[k : k + 1, :] for k in range(4)]
    hots = [(r == label).astype(F32) for r in rows]
    hot = hots[0] + hots[1] + hots[2] + hots[3]
    before = jnp.dot(hot.astype(BF), earlier, preferred_element_type=F32)
    spilled, seconds, second_hots, first_ranks = [], [], [], []
    for k in range(4):
        rank = jnp.sum(before * hots[k], axis=0, keepdims=True)
        limit = jnp.sum(lim * hots[k], axis=0, keepdims=True)
        spill = rank >= limit
        second = (rows[k] + shifts[k : k + 1, :]) & 63
        first_ranks.append(rank)
        spilled.append(spill)
        seconds.append(second)
        second_hots.append((second == label).astype(F32))
    spill_hots = [h * s.astype(F32) for h, s in zip(second_hots, spilled)]
    total = spill_hots[0] + spill_hots[1] + spill_hots[2] + spill_hots[3]
    run = jnp.dot(total.astype(BF), earlier, preferred_element_type=F32)
    out = []
    for k in range(4):
        rank = jnp.sum(run * second_hots[k], axis=0, keepdims=True)
        run = run + spill_hots[k]
        limit = jnp.sum(lim * second_hots[k], axis=0, keepdims=True)
        slot = jnp.where(spilled[k], limit + rank, first_ranks[k]).astype(jnp.int32)
        target = jnp.where(spilled[k], seconds[k], rows[k])
        out.append((target, slot, slot < CAP))
    return out


def place_kernel(tok_ref, ids_ref, shift_ref, raw_ref, lim_ref, out_ref):
    out_ref[:2880, :] = tok_ref[...]
    places = place(ids_ref[...], shift_ref[...], lim_ref[...])
    raw = raw_ref[...]
    share = raw / jnp.sum(raw, axis=0, keepdims=True)
    rows = [t.astype(F32) for t, _, _ in places]
    rows += [jnp.where(k, s, -1).astype(F32) for _, s, k in places]
    rows += [share, jnp.zeros((4, 128), F32)]
    out_ref[2880:, :] = jnp.concatenate(rows, axis=0).astype(BF)


def place_call(tok, ids, shifts, raw, lim):
    vm = pl.BlockSpec(memory_space=pltpu.VMEM)
    return pl.pallas_call(
        place_kernel,
        in_specs=[vm] * 5,
        out_specs=vm,
        out_shape=jax.ShapeDtypeStruct((2896, 128), BF),
        compiler_params=pltpu.CompilerParams(vmem_limit_bytes=16 << 20),
        cost_estimate=pl.CostEstimate(flops=1 << 22, bytes_accessed=1_500_000, transcendentals=0),
        name="place",
    )(tok, ids, shifts, raw, lim)


def slots_of(tail, core):
    tail = tail.astype(F32)
    out = []
    for k in range(4):
        target = tail[k : k + 1].astype(jnp.int32)
        slot = tail[4 + k : 5 + k].astype(jnp.int32)
        mine = (slot >= 0) & (((target >> 2) & 1) == core)
        out.append((mine, (target >> 3) * 4 + (target & 3), slot, tail[8 + k : 9 + k]))
    return out


def row_weights(tail, core, side, chunk, weighted):
    low, size = ((0, 8), (8, 16))[chunk]
    at = lax.broadcasted_iota(jnp.int32, (32 * size, 128), 0)
    total = jnp.zeros((32 * size, 128), F32)
    for mine, index, slot, share in slots_of(tail, core):
        row = slot + (side * CAP - low)
        row = jnp.where(mine & (row >= 0) & (row < size), index * size + row, -1)
        total = total + jnp.where(row == at, share if weighted else 1.0, 0.0)
    return total


def rows0_kernel(at_ref, own_ref, out_ref):
    hot = row_weights(own_ref[2880:, :], at_ref[0], 0, 0, False).astype(BF)
    got = lax.dot_general(hot, own_ref[:2880, :], NT, preferred_element_type=F32).astype(BF)
    out_ref[0] = got
    out_ref[1] = got


def rows0(at, own):
    vm = pl.BlockSpec(memory_space=pltpu.VMEM)
    return pl.pallas_call(
        rows0_kernel,
        grid=(1,),
        in_specs=[pl.BlockSpec(memory_space=pltpu.SMEM), vm],
        out_specs=pl.BlockSpec((2, 256, 2880), lambda i: (0, 0, 0)),
        out_shape=pltpu.HBM((2, 256, 2880), BF),
        compiler_params=pltpu.CompilerParams(vmem_limit_bytes=32 << 20),
        cost_estimate=pl.CostEstimate(flops=2 * 256 * 128 * 2880, bytes_accessed=3_700_000, transcendentals=0),
        name="rows0",
    )(at, own)


def rows1_kernel(at_ref, own_ref, sib_ref, out_ref, hot_ref):
    step = pl.program_id(0)

    @pl.when(step == 0)
    def _():
        for side, ref in enumerate((own_ref, sib_ref)):
            hot_ref[:, 128 * side : 128 * side + 128] = row_weights(
                ref[2880:, :], at_ref[0], side, 1, False
            ).astype(BF)

    both = jnp.concatenate([own_ref[:2880, :], sib_ref[:2880, :]], axis=1)
    hot = hot_ref[pl.ds(pl.multiple_of(step * 256, 256), 256), :]
    got = lax.dot_general(hot, both, NT, preferred_element_type=F32).astype(BF)
    out_ref[0] = got
    out_ref[1] = got


def rows1(at, own, sib):
    vm = pl.BlockSpec(memory_space=pltpu.VMEM)
    return pl.pallas_call(
        rows1_kernel,
        grid=(2,),
        in_specs=[pl.BlockSpec(memory_space=pltpu.SMEM), vm, vm],
        out_specs=pl.BlockSpec((2, 256, 2880), lambda i: (0, i, 0)),
        out_shape=pltpu.HBM((2, 512, 2880), BF),
        scratch_shapes=[pltpu.VMEM((512, 256), BF)],
        compiler_params=pltpu.CompilerParams(vmem_limit_bytes=32 << 20),
        cost_estimate=pl.CostEstimate(flops=2 * 512 * 256 * 2880, bytes_accessed=7_400_000, transcendentals=0),
        name="rows1",
    )(at, own, sib)


def ffn_kernel(x_ref, g_hbm, u_hbm, d_hbm, out_ref, g_ref, u_ref, d_ref, sems):
    step = pl.program_id(0)
    copies = [
        pltpu.make_async_copy(g_hbm.at[0], g_ref, sems.at[0]),
        pltpu.make_async_copy(u_hbm.at[0], u_ref, sems.at[1]),
        pltpu.make_async_copy(d_hbm, d_ref, sems.at[2]),
    ]

    @pl.when(step == 0)
    def _():
        for c in copies:
            c.start()
        copies[0].wait()

    x = x_ref[...]
    gating = jnp.dot(x, g_ref[...], preferred_element_type=F32)

    @pl.when(step == 0)
    def _():
        copies[1].wait()

    upward = jnp.dot(x, u_ref[...], preferred_element_type=F32)
    active = ((upward + 1.0) * gating * jax.nn.sigmoid(1.702 * gating)).astype(BF)

    @pl.when(step == 0)
    def _():
        copies[2].wait()

    out_ref[...] = lax.dot_general(active, d_ref[...], NT, preferred_element_type=F32).astype(BF)


def ffn(x, g, u, d_t):
    count = x.shape[0]
    hbm = pl.BlockSpec(memory_space=pltpu.HBM)
    held = pltpu.VMEM((2880, 768), BF)
    return pl.pallas_call(
        ffn_kernel,
        grid=(count // 512,),
        in_specs=[pl.BlockSpec((512, 2880), lambda i: (i, 0)), hbm, hbm, hbm],
        out_specs=pl.BlockSpec((512, 2880), lambda i: (i, 0)),
        out_shape=pltpu.HBM((count, 2880), BF),
        scratch_shapes=[held, held, held, pltpu.SemaphoreType.DMA((3,))],
        compiler_params=pltpu.CompilerParams(vmem_limit_bytes=58 << 20),
        cost_estimate=pl.CostEstimate(
            flops=6 * count * 2880 * 768, bytes_accessed=13_300_000 + count * 2880 * 4, transcendentals=count * 768
        ),
        name="ffn%d" % count,
    )(x, g, u, d_t)


def combine0_kernel(at_ref, y_ref, tail_ref, out_ref):
    w = row_weights(tail_ref[...], at_ref[0], 0, 0, True).T.astype(BF)
    out_ref[...] = jnp.dot(w, y_ref[0], preferred_element_type=F32) + jnp.dot(
        w, y_ref[1], preferred_element_type=F32
    )


def combine0(at, y, tail):
    vm = pl.BlockSpec(memory_space=pltpu.VMEM)
    return pl.pallas_call(
        combine0_kernel,
        in_specs=[pl.BlockSpec(memory_space=pltpu.SMEM), vm, vm],
        out_specs=vm,
        out_shape=jax.ShapeDtypeStruct((128, 2880), F32),
        compiler_params=pltpu.CompilerParams(vmem_limit_bytes=24 << 20),
        cost_estimate=pl.CostEstimate(flops=4 * 256 * 128 * 2880, bytes_accessed=4_400_000, transcendentals=0),
        name="combine0",
    )(at, y, tail)


def combine1_kernel(at_ref, y_ref, own_tail_ref, sib_tail_ref, first_ref, own_ref, sib_ref, w_ref, acc_ref):
    step = pl.program_id(0)

    @pl.when(step == 0)
    def _():
        for side, ref in enumerate((own_tail_ref, sib_tail_ref)):
            w = row_weights(ref[...], at_ref[0], side, 1, True).T.astype(BF)
            for b in range(4):
                w_ref[b, 128 * side : 128 * side + 128, :] = w[:, 128 * b : 128 * b + 128]
        acc_ref[:128, :] = first_ref[...]
        acc_ref[128:, :] = jnp.zeros((128, 2880), F32)

    w = w_ref[step]
    acc_ref[...] += jnp.dot(w, y_ref[0], preferred_element_type=F32) + jnp.dot(
        w, y_ref[1], preferred_element_type=F32
    )

    @pl.when(step == 3)
    def _():
        own_ref[...] = acc_ref[:128, :].T
        sib_ref[...] = acc_ref[128:, :].T.astype(BF)


def combine1(at, y, own_tail, sib_tail, first):
    vm = pl.BlockSpec(memory_space=pltpu.VMEM)
    return pl.pallas_call(
        combine1_kernel,
        grid=(4,),
        in_specs=[
            pl.BlockSpec(memory_space=pltpu.SMEM),
            pl.BlockSpec((2, 128, 2880), lambda i: (0, i, 0)),
            vm,
            vm,
            vm,
        ],
        out_specs=[pl.BlockSpec((2880, 128), lambda i: (0, 0))] * 2,
        out_shape=[jax.ShapeDtypeStruct((2880, 128), F32), jax.ShapeDtypeStruct((2880, 128), BF)],
        scratch_shapes=[pltpu.VMEM((4, 256, 128), BF), pltpu.VMEM((256, 2880), F32)],
        compiler_params=pltpu.CompilerParams(vmem_limit_bytes=48 << 20),
        cost_estimate=pl.CostEstimate(flops=4 * 512 * 256 * 2880, bytes_accessed=9_000_000, transcendentals=0),
        name="combine1",
    )(at, y, own_tail, sib_tail, first)


def grad_kernel(at_ref, p0_ref, p1_ref, p2_ref, p3_ref, mine_ref, far_ref, out_ref):
    y, x = at_ref[1], at_ref[3]
    total = None
    for o, (one, two) in ((0, (p0_ref, p1_ref)), (2, (p2_ref, p3_ref))):
        right = [
            jnp.concatenate([mine_ref[(y + o + i) & 3], far_ref[(y + o + i) & 3]], axis=1) for i in range(2)
        ]
        left = jnp.concatenate([one[...], two[...]], axis=1)
        term = jnp.dot(left, jnp.concatenate(right, axis=0), preferred_element_type=F32)
        total = term if total is None else total + term
    for j in range(4):
        for side in range(2):
            low = 512 * side + 128 * j
            out_ref[0, pl.ds((j - x) & 3, 1), 0, side] = total[None, :, low : low + 128].astype(BF)


def local_grad(at, blocks, mine, far):
    vm = pl.BlockSpec(memory_space=pltpu.VMEM)
    return pl.pallas_call(
        grad_kernel,
        grid_spec=pltpu.PrefetchScalarGridSpec(
            num_scalar_prefetch=1,
            grid=(4,),
            in_specs=[pl.BlockSpec((720, 128), lambda i, at: (i, 0))] * 4 + [vm, vm],
            out_specs=pl.BlockSpec(
                (1, 4, 1, 2, 720, 128), lambda i, at: ((i >> 1) ^ at[0], 0, (i & 1) ^ at[4], 0, 0, 0)
            ),
        ),
        out_shape=jax.ShapeDtypeStruct((2, 4, 2, 2, 720, 128), BF),
        compiler_params=pltpu.CompilerParams(vmem_limit_bytes=32 << 20),
        cost_estimate=pl.CostEstimate(flops=2 * 1024 * 512 * 2880, bytes_accessed=10_000_000, transcendentals=0),
        name="local_grad",
    )(at, *blocks, mine, far)


def spread_kernel(at_ref, own_ref, sib_ref, out_ref):
    core = at_ref[0]
    out_ref[pl.ds(core, 1)] = own_ref[...].astype(F32)
    out_ref[pl.ds(1 - core, 1)] = sib_ref[...].astype(F32)


def spread(at, own, sib):
    block = pl.BlockSpec((1, 1440, 128), lambda i, at: (i, 0, 0))
    return pl.pallas_call(
        spread_kernel,
        grid_spec=pltpu.PrefetchScalarGridSpec(
            num_scalar_prefetch=1,
            grid=(4,),
            in_specs=[block, block],
            out_specs=pl.BlockSpec((2, 1440, 128), lambda i, at: (0, 0, (at[3] + i) & 3)),
        ),
        out_shape=jax.ShapeDtypeStruct((2, 1440, 512), F32),
        compiler_params=pltpu.CompilerParams(vmem_limit_bytes=16 << 20),
        cost_estimate=pl.CostEstimate(flops=0, bytes_accessed=9_000_000, transcendentals=0),
        name="spread",
    )(at, own, sib)


def shift(axis, by, n):
    return functools.partial(lax.ppermute, axis_name=axis, perm=[(i, (i + by) % n) for i in range(n)])


def from_others(block, axis):
    return [shift(axis, -o, 4)(block) for o in (1, 2, 3)]


def after(value, *others):
    return lax.optimization_barrier((value,) + others)[0]


def toward(o, q):
    perm = [(i, (((i >> 1) + o) & 3) * 2 + ((i & 1) ^ q)) for i in range(8)]
    return functools.partial(lax.ppermute, axis_name=("x", "zh"), perm=perm)


OTHERS = [(o, q) for o in range(4) for q in range(2) if (o, q) != (0, 0)]


def local(tokens, expert_ids, gate_raw, overflow_shift, limits, gate_w, up_w, down_w, context, out_grad):
    at = jnp.stack([lax.axis_index(a) for a in ("core", "y", "zl", "x", "zh")]).astype(jnp.int32)
    zh, zl = lax.axis_index("zh"), lax.axis_index("zl")
    core_swap, zl_swap = shift("core", 1, 2), shift("zl", 1, 2)
    over = ("zl", "x", "zh", "y")
    weights = gate_w, up_w, down_w[0].T

    def exchange(rows):
        return lax.all_to_all(rows.reshape(64, -1, 2880), over, split_axis=0, concat_axis=0, tiled=True)

    lim = jnp.broadcast_to(limits.astype(F32)[:, None], (64, 128))
    mine = place_call(tokens.T, expert_ids.T, overflow_shift.T, gate_raw.T, lim)
    got0 = exchange(rows0(at, mine)).reshape(512, 2880)
    sibling = core_swap(mine)

    og = out_grad.T
    ogs = from_others(og, "y")
    ctx = context.reshape(4, 2, 128, 512)
    ctx_mine = lax.dynamic_index_in_dim(ctx, zl, 1, keepdims=False)
    ctx_far = zl_swap(lax.dynamic_index_in_dim(ctx, 1 - zl, 1, keepdims=False))
    send1 = after(rows1(at, mine, sibling), got0, ctx_far, *ogs)
    got1 = exchange(send1).reshape(1024, 2880)

    out0 = ffn(got0, *weights)
    grads = local_grad(at, [og] + ogs, ctx_mine, ctx_far)
    part = grads[0].astype(F32) + core_swap(grads[1]).astype(F32)
    terms = [toward(o, q)(part[o, q].astype(BF)) for o, q in OTHERS]
    back0 = exchange(after(out0, got1, part))
    out1 = ffn(got1, *weights)

    total = part[0, 0]
    for term in terms:
        total = total + term.astype(F32)
    final = (total[0] + zl_swap(total[1].astype(BF)).astype(F32)).astype(BF)
    back1 = exchange(after(out1, back0, final))
    first = combine0(at, back0.reshape(2, 256, 2880), mine[2880:])

    come = {(0, 0): final}
    for o, q in OTHERS:
        come[o, q] = toward(-o, q)(final)
    pieces = []
    for o in range(4):
        same, other = come[o, 0], come[o, 1]
        pieces.append(jnp.concatenate([jnp.where(zh == 0, same, other), jnp.where(zh == 0, other, same)]))
    full = jnp.stack(pieces)
    grad = spread(at, full, core_swap(full)).reshape(2880, 512)

    own, sib = combine1(at, back1.reshape(2, 512, 2880), mine[2880:], sibling[2880:], first)
    mixed = (own + core_swap(sib).astype(F32)).astype(BF)
    return mixed.T, grad.T


def solution(mesh):
    fine = Mesh(mesh.devices.reshape(4, 2, 2, 4, 2), ("x", "zh", "core", "y", "zl"))
    every = ("x", "zh", "core", "y", "zl")
    two, three = P(every, None), P(every, None, None)
    in_specs = (two, two, two, two, P(), three, three, three, P(("x", "zh", "core"), ("y", "zl")), two)
    out_specs = (two, P(("y", "zl"), None))
    return jax.shard_map(local, mesh=fine, in_specs=in_specs, out_specs=out_specs, check_vma=False)
```

```python
import functools

import jax
import jax.numpy as jnp
from jax import lax
from jax.experimental import pallas as pl
from jax.experimental.pallas import tpu as pltpu
from jax.sharding import Mesh, PartitionSpec as P

CAP = 12
BF = jnp.bfloat16
F32 = jnp.float32
NT = (((1,), (1,)), ((), ()))


def place(ids, shifts, lim):
    label = lax.broadcasted_iota(jnp.int32, (64, 128), 0)
    earlier = (
        lax.broadcasted_iota(jnp.int32, (128, 128), 0)
        < lax.broadcasted_iota(jnp.int32, (128, 128), 1)
    ).astype(F32).astype(BF)
    rows = [ids[k : k + 1, :] for k in range(4)]
    hots = [(r == label).astype(F32) for r in rows]
    hot = hots[0] + hots[1] + hots[2] + hots[3]
    before = jnp.dot(hot.astype(BF), earlier, preferred_element_type=F32)
    spilled, seconds, second_hots, first_ranks = [], [], [], []
    for k in range(4):
        rank = jnp.sum(before * hots[k], axis=0, keepdims=True)
        limit = jnp.sum(lim * hots[k], axis=0, keepdims=True)
        spill = rank >= limit
        second = (rows[k] + shifts[k : k + 1, :]) & 63
        first_ranks.append(rank)
        spilled.append(spill)
        seconds.append(second)
        second_hots.append((second == label).astype(F32))
    spill_hots = [h * s.astype(F32) for h, s in zip(second_hots, spilled)]
    total = spill_hots[0] + spill_hots[1] + spill_hots[2] + spill_hots[3]
    run = jnp.dot(total.astype(BF), earlier, preferred_element_type=F32)
    out = []
    for k in range(4):
        rank = jnp.sum(run * second_hots[k], axis=0, keepdims=True)
        run = run + spill_hots[k]
        limit = jnp.sum(lim * second_hots[k], axis=0, keepdims=True)
        slot = jnp.where(spilled[k], limit + rank, first_ranks[k]).astype(jnp.int32)
        target = jnp.where(spilled[k], seconds[k], rows[k])
        out.append((target, slot, slot < CAP))
    return out


def place_kernel(tok_ref, ids_ref, shift_ref, raw_ref, lim_ref, out_ref):
    out_ref[:2880, :] = tok_ref[...]
    places = place(ids_ref[...], shift_ref[...], lim_ref[...])
    raw = raw_ref[...]
    share = raw / jnp.sum(raw, axis=0, keepdims=True)
    rows = [t.astype(F32) for t, _, _ in places]
    rows += [jnp.where(k, s, -1).astype(F32) for _, s, k in places]
    rows += [share, jnp.zeros((4, 128), F32)]
    out_ref[2880:, :] = jnp.concatenate(rows, axis=0).astype(BF)


def place_call(tok, ids, shifts, raw, lim):
    vm = pl.BlockSpec(memory_space=pltpu.VMEM)
    return pl.pallas_call(
        place_kernel,
        in_specs=[vm] * 5,
        out_specs=vm,
        out_shape=jax.ShapeDtypeStruct((2896, 128), BF),
        compiler_params=pltpu.CompilerParams(vmem_limit_bytes=16 << 20),
        cost_estimate=pl.CostEstimate(flops=1 << 22, bytes_accessed=1_500_000, transcendentals=0),
        name="place",
    )(tok, ids, shifts, raw, lim)


def slots_of(tail, core):
    tail = tail.astype(F32)
    out = []
    for k in range(4):
        target = tail[k : k + 1].astype(jnp.int32)
        slot = tail[4 + k : 5 + k].astype(jnp.int32)
        mine = (slot >= 0) & (((target >> 2) & 1) == core)
        out.append((mine, (target >> 3) * 4 + (target & 3), slot, tail[8 + k : 9 + k]))
    return out


def row_weights(tail, core, side, weighted):
    at = lax.broadcasted_iota(jnp.int32, (768, 128), 0)
    total = jnp.zeros((768, 128), F32)
    for mine, index, slot, share in slots_of(tail, core):
        row = jnp.where(mine, index * 24 + side * CAP + slot, -1)
        total = total + jnp.where(row == at, share if weighted else 1.0, 0.0)
    return total


def rows_kernel(at_ref, own_ref, sib_ref, out_ref, hot_ref):
    step = pl.program_id(0)

    @pl.when(step == 0)
    def _():
        for side, ref in enumerate((own_ref, sib_ref)):
            hot_ref[:, 128 * side : 128 * side + 128] = row_weights(ref[2880:, :], at_ref[0], side, False).astype(BF)

    both = jnp.concatenate([own_ref[:2880, :], sib_ref[:2880, :]], axis=1)
    hot = hot_ref[pl.ds(pl.multiple_of(step * 256, 256), 256), :]
    got = lax.dot_general(hot, both, NT, preferred_element_type=F32).astype(BF)
    out_ref[0] = got
    out_ref[1] = got


def rows_of(at, own, sib):
    vm = pl.BlockSpec(memory_space=pltpu.VMEM)
    return pl.pallas_call(
        rows_kernel,
        grid=(3,),
        in_specs=[pl.BlockSpec(memory_space=pltpu.SMEM), vm, vm],
        out_specs=pl.BlockSpec((2, 256, 2880), lambda i: (0, i, 0)),
        out_shape=pltpu.HBM((2, 768, 2880), BF),
        scratch_shapes=[pltpu.VMEM((768, 256), BF)],
        compiler_params=pltpu.CompilerParams(vmem_limit_bytes=32 << 20),
        cost_estimate=pl.CostEstimate(flops=2 * 768 * 256 * 2880, bytes_accessed=10_000_000, transcendentals=0),
        name="rows",
    )(at, own, sib)


def ffn_kernel(x_ref, g_hbm, u_hbm, d_hbm, out_ref, g_ref, u_ref, d_ref, sems):
    step = pl.program_id(0)
    copies = [
        pltpu.make_async_copy(g_hbm.at[0], g_ref, sems.at[0]),
        pltpu.make_async_copy(u_hbm.at[0], u_ref, sems.at[1]),
        pltpu.make_async_copy(d_hbm, d_ref, sems.at[2]),
    ]

    @pl.when(step == 0)
    def _():
        for c in copies:
            c.start()
        copies[0].wait()

    x = x_ref[...]
    gating = jnp.dot(x, g_ref[...], preferred_element_type=F32)

    @pl.when(step == 0)
    def _():
        copies[1].wait()

    upward = jnp.dot(x, u_ref[...], preferred_element_type=F32)
    active = ((upward + 1.0) * gating * jax.nn.sigmoid(1.702 * gating)).astype(BF)

    @pl.when(step == 0)
    def _():
        copies[2].wait()

    out_ref[...] = lax.dot_general(active, d_ref[...], NT, preferred_element_type=F32).astype(BF)


def ffn(x, g, u, d_t):
    count = x.shape[0]
    hbm = pl.BlockSpec(memory_space=pltpu.HBM)
    held = pltpu.VMEM((2880, 768), BF)
    return pl.pallas_call(
        ffn_kernel,
        grid=(count // 512,),
        in_specs=[pl.BlockSpec((512, 2880), lambda i: (i, 0)), hbm, hbm, hbm],
        out_specs=pl.BlockSpec((512, 2880), lambda i: (i, 0)),
        out_shape=pltpu.HBM((count, 2880), BF),
        scratch_shapes=[held, held, held, pltpu.SemaphoreType.DMA((3,))],
        compiler_params=pltpu.CompilerParams(vmem_limit_bytes=58 << 20),
        cost_estimate=pl.CostEstimate(
            flops=6 * count * 2880 * 768, bytes_accessed=13_300_000 + count * 2880 * 4, transcendentals=count * 768
        ),
        name="ffn%d" % count,
    )(x, g, u, d_t)


def combine_kernel(at_ref, y_ref, own_tail_ref, sib_tail_ref, own_ref, sib_ref, w_ref, acc_ref):
    step = pl.program_id(0)

    @pl.when(step == 0)
    def _():
        for side, ref in enumerate((own_tail_ref, sib_tail_ref)):
            w = row_weights(ref[...], at_ref[0], side, True).T.astype(BF)
            for b in range(6):
                w_ref[b, 128 * side : 128 * side + 128, :] = w[:, 128 * b : 128 * b + 128]
        acc_ref[...] = jnp.zeros_like(acc_ref)

    w = w_ref[step]
    acc_ref[...] += jnp.dot(w, y_ref[0], preferred_element_type=F32) + jnp.dot(
        w, y_ref[1], preferred_element_type=F32
    )

    @pl.when(step == 5)
    def _():
        own_ref[...] = acc_ref[:128, :].T
        sib_ref[...] = acc_ref[128:, :].T.astype(BF)


def combine(at, y, own_tail, sib_tail):
    vm = pl.BlockSpec(memory_space=pltpu.VMEM)
    return pl.pallas_call(
        combine_kernel,
        grid=(6,),
        in_specs=[
            pl.BlockSpec(memory_space=pltpu.SMEM),
            pl.BlockSpec((2, 128, 2880), lambda i: (0, i, 0)),
            vm,
            vm,
        ],
        out_specs=[pl.BlockSpec((2880, 128), lambda i: (0, 0))] * 2,
        out_shape=[jax.ShapeDtypeStruct((2880, 128), F32), jax.ShapeDtypeStruct((2880, 128), BF)],
        scratch_shapes=[pltpu.VMEM((6, 256, 128), BF), pltpu.VMEM((256, 2880), F32)],
        compiler_params=pltpu.CompilerParams(vmem_limit_bytes=48 << 20),
        cost_estimate=pl.CostEstimate(flops=4 * 768 * 256 * 2880, bytes_accessed=12_000_000, transcendentals=0),
        name="combine",
    )(at, y, own_tail, sib_tail)


def grad_kernel(at_ref, og_ref, mine_ref, far_ref, out_ref):
    zl = at_ref[2]
    total = None
    for o in (0, 2):
        right = [jnp.concatenate([mine_ref[o + i], far_ref[o + i]], axis=1) for i in range(2)]
        left = jnp.concatenate([og_ref[o], og_ref[o + 1]], axis=1)
        term = jnp.dot(left, jnp.concatenate(right, axis=0), preferred_element_type=F32)
        total = term if total is None else total + term
    for j in range(4):
        for side in range(2):
            low = 512 * side + 128 * j
            out_ref[0, j, 0, pl.ds(side ^ zl, 1)] = total[None, :, low : low + 128].astype(BF)


def local_grad(at, og, mine, far):
    vm = pl.BlockSpec(memory_space=pltpu.VMEM)
    return pl.pallas_call(
        grad_kernel,
        grid_spec=pltpu.PrefetchScalarGridSpec(
            num_scalar_prefetch=1,
            grid=(4,),
            in_specs=[pl.BlockSpec((4, 720, 128), lambda i, at: (0, i, 0)), vm, vm],
            out_specs=pl.BlockSpec((1, 4, 1, 2, 720, 128), lambda i, at: ((i >> 1) ^ at[0], 0, i & 1, 0, 0, 0)),
        ),
        out_shape=jax.ShapeDtypeStruct((2, 4, 2, 2, 720, 128), BF),
        compiler_params=pltpu.CompilerParams(vmem_limit_bytes=32 << 20),
        cost_estimate=pl.CostEstimate(flops=2 * 1024 * 512 * 2880, bytes_accessed=10_000_000, transcendentals=0),
        name="local_grad",
    )(at, og, mine, far)


def spread_kernel(at_ref, own_ref, sib_ref, out_ref):
    core = at_ref[0]
    out_ref[pl.ds(core, 1)] = own_ref[...].astype(F32)
    out_ref[pl.ds(1 - core, 1)] = sib_ref[...].astype(F32)


def spread(at, own, sib):
    block = pl.BlockSpec((1, 1440, 128), lambda i, at: (i, 0, 0))
    return pl.pallas_call(
        spread_kernel,
        grid_spec=pltpu.PrefetchScalarGridSpec(
            num_scalar_prefetch=1,
            grid=(4,),
            in_specs=[block, block],
            out_specs=pl.BlockSpec((2, 1440, 128), lambda i, at: (0, 0, i)),
        ),
        out_shape=jax.ShapeDtypeStruct((2, 1440, 512), F32),
        compiler_params=pltpu.CompilerParams(vmem_limit_bytes=16 << 20),
        cost_estimate=pl.CostEstimate(flops=0, bytes_accessed=9_000_000, transcendentals=0),
        name="spread",
    )(at, own, sib)


def shift(axis, by, n):
    return functools.partial(lax.ppermute, axis_name=axis, perm=[(i, (i + by) % n) for i in range(n)])


def after(value, *others):
    return lax.optimization_barrier((value,) + others)[0]


def local(tokens, expert_ids, gate_raw, overflow_shift, limits, gate_w, up_w, down_w, context, out_grad):
    at = jnp.stack([lax.axis_index(a) for a in ("core", "y", "zl", "x", "zh")]).astype(jnp.int32)
    zl = lax.axis_index("zl")
    core_swap, zl_swap = shift("core", 1, 2), shift("zl", 1, 2)
    over = ("zl", "x", "zh", "y")

    def exchange(rows):
        return lax.all_to_all(rows.reshape(64, 24, 2880), over, split_axis=0, concat_axis=0, tiled=True)

    og = lax.all_gather(out_grad.T, "y", axis=0)
    ctx = context.reshape(4, 2, 128, 512)
    ctx_mine = lax.dynamic_index_in_dim(ctx, zl, 1, keepdims=False)
    ctx_far = zl_swap(lax.dynamic_index_in_dim(ctx, 1 - zl, 1, keepdims=False))

    lim = jnp.broadcast_to(limits.astype(F32)[:, None], (64, 128))
    mine = place_call(tokens.T, expert_ids.T, overflow_shift.T, gate_raw.T, lim)
    sibling = core_swap(mine)
    got = exchange(after(rows_of(at, mine, sibling), ctx_far)).reshape(1536, 2880)

    grads = local_grad(at, og, ctx_mine, ctx_far)
    part = (grads[0].astype(F32) + core_swap(grads[1]).astype(F32)).astype(BF)
    own_part = lax.psum_scatter(
        part.reshape(16 * 720, 128), ("x", "zh", "zl"), scatter_dimension=0, tiled=True
    )
    out = ffn(after(got, part), gate_w, up_w, down_w[0].T)
    back = exchange(out)
    full = lax.all_gather(after(own_part, out), ("x", "zh"), axis=0, tiled=True).reshape(4, 1440, 128)
    grad = spread(at, full, core_swap(full)).reshape(2880, 512)

    own, sib = combine(at, back.reshape(2, 768, 2880), mine[2880:], sibling[2880:])
    mixed = (own + core_swap(sib).astype(F32)).astype(BF)
    return mixed.T, grad.T


def solution(mesh):
    fine = Mesh(mesh.devices.reshape(4, 2, 2, 4, 2), ("x", "zh", "core", "y", "zl"))
    every = ("x", "zh", "core", "y", "zl")
    two, three = P(every, None), P(every, None, None)
    in_specs = (two, two, two, two, P(), three, three, three, P(("x", "zh", "core"), ("y", "zl")), two)
    out_specs = (two, P(("y", "zl"), None))
    return jax.shard_map(local, mesh=fine, in_specs=in_specs, out_specs=out_specs, check_vma=False)
```

```python
import functools

import jax
import jax.numpy as jnp
from jax import lax
from jax.experimental import pallas as pl
from jax.experimental.pallas import tpu as pltpu
from jax.sharding import Mesh, PartitionSpec as P

CAP = 12
BF = jnp.bfloat16
F32 = jnp.float32
NT = (((1,), (1,)), ((), ()))


def place(ids, shifts, lim):
    label = lax.broadcasted_iota(jnp.int32, (64, 128), 0)
    earlier = (
        lax.broadcasted_iota(jnp.int32, (128, 128), 0)
        < lax.broadcasted_iota(jnp.int32, (128, 128), 1)
    ).astype(F32).astype(BF)
    rows = [ids[k : k + 1, :] for k in range(4)]
    hots = [(r == label).astype(F32) for r in rows]
    hot = hots[0] + hots[1] + hots[2] + hots[3]
    before = jnp.dot(hot.astype(BF), earlier, preferred_element_type=F32)
    spilled, seconds, second_hots, first_ranks = [], [], [], []
    for k in range(4):
        rank = jnp.sum(before * hots[k], axis=0, keepdims=True)
        limit = jnp.sum(lim * hots[k], axis=0, keepdims=True)
        spill = rank >= limit
        second = (rows[k] + shifts[k : k + 1, :]) & 63
        first_ranks.append(rank)
        spilled.append(spill)
        seconds.append(second)
        second_hots.append((second == label).astype(F32))
    spill_hots = [h * s.astype(F32) for h, s in zip(second_hots, spilled)]
    total = spill_hots[0] + spill_hots[1] + spill_hots[2] + spill_hots[3]
    run = jnp.dot(total.astype(BF), earlier, preferred_element_type=F32)
    out = []
    for k in range(4):
        rank = jnp.sum(run * second_hots[k], axis=0, keepdims=True)
        run = run + spill_hots[k]
        limit = jnp.sum(lim * second_hots[k], axis=0, keepdims=True)
        slot = jnp.where(spilled[k], limit + rank, first_ranks[k]).astype(jnp.int32)
        target = jnp.where(spilled[k], seconds[k], rows[k])
        out.append((target, slot, slot < CAP))
    return out


def place_kernel(tok_ref, ids_ref, shift_ref, raw_ref, lim_ref, out_ref):
    out_ref[:2880, :] = tok_ref[...]
    places = place(ids_ref[...], shift_ref[...], lim_ref[...])
    raw = raw_ref[...]
    share = raw / jnp.sum(raw, axis=0, keepdims=True)
    rows = [t.astype(F32) for t, _, _ in places]
    rows += [jnp.where(k, s, -1).astype(F32) for _, s, k in places]
    rows += [share, jnp.zeros((4, 128), F32)]
    out_ref[2880:, :] = jnp.concatenate(rows, axis=0).astype(BF)


def place_call(tok, ids, shifts, raw, lim):
    vm = pl.BlockSpec(memory_space=pltpu.VMEM)
    return pl.pallas_call(
        place_kernel,
        in_specs=[vm] * 5,
        out_specs=vm,
        out_shape=jax.ShapeDtypeStruct((2896, 128), BF),
        compiler_params=pltpu.CompilerParams(vmem_limit_bytes=16 << 20),
        cost_estimate=pl.CostEstimate(flops=1 << 22, bytes_accessed=1_500_000, transcendentals=0),
        name="place",
    )(tok, ids, shifts, raw, lim)


def slots_of(tail, core):
    tail = tail.astype(F32)
    out = []
    for k in range(4):
        target = tail[k : k + 1].astype(jnp.int32)
        slot = tail[4 + k : 5 + k].astype(jnp.int32)
        mine = (slot >= 0) & (((target >> 2) & 1) == core)
        out.append((mine, (target >> 3) * 4 + (target & 3), slot, tail[8 + k : 9 + k]))
    return out


def row_weights(tail, core, side, weighted):
    at = lax.broadcasted_iota(jnp.int32, (768, 128), 0)
    total = jnp.zeros((768, 128), F32)
    for mine, index, slot, share in slots_of(tail, core):
        row = jnp.where(mine, index * 24 + side * CAP + slot, -1)
        total = total + jnp.where(row == at, share if weighted else 1.0, 0.0)
    return total


def rows_kernel(at_ref, own_ref, sib_ref, out_ref, hot_ref):
    step = pl.program_id(0)

    @pl.when(step == 0)
    def _():
        for side, ref in enumerate((own_ref, sib_ref)):
            hot_ref[:, 128 * side : 128 * side + 128] = row_weights(ref[2880:, :], at_ref[0], side, False).astype(BF)

    both = jnp.concatenate([own_ref[:2880, :], sib_ref[:2880, :]], axis=1)
    hot = hot_ref[pl.ds(pl.multiple_of(step * 256, 256), 256), :]
    got = lax.dot_general(hot, both, NT, preferred_element_type=F32).astype(BF)
    out_ref[0] = got
    out_ref[1] = got


def rows_of(at, own, sib):
    vm = pl.BlockSpec(memory_space=pltpu.VMEM)
    return pl.pallas_call(
        rows_kernel,
        grid=(3,),
        in_specs=[pl.BlockSpec(memory_space=pltpu.SMEM), vm, vm],
        out_specs=pl.BlockSpec((2, 256, 2880), lambda i: (0, i, 0)),
        out_shape=pltpu.HBM((2, 768, 2880), BF),
        scratch_shapes=[pltpu.VMEM((768, 256), BF)],
        compiler_params=pltpu.CompilerParams(vmem_limit_bytes=32 << 20),
        cost_estimate=pl.CostEstimate(flops=2 * 768 * 256 * 2880, bytes_accessed=10_000_000, transcendentals=0),
        name="rows",
    )(at, own, sib)


def ffn_rows(x, g_ref, u_ref, d_ref, copies=()):
    for c in copies[:1]:
        c.wait()
    gating = jnp.dot(x, g_ref[...], preferred_element_type=F32)
    for c in copies[1:2]:
        c.wait()
    upward = jnp.dot(x, u_ref[...], preferred_element_type=F32)
    active = ((upward + 1.0) * gating * jax.nn.sigmoid(1.702 * gating)).astype(BF)
    for c in copies[2:]:
        c.wait()
    return lax.dot_general(active, d_ref[...], NT, preferred_element_type=F32).astype(BF)


def first_kernel(x_ref, g_hbm, u_hbm, d_hbm, out_ref, g_ref, u_ref, d_ref, sems):
    @pl.when(pl.program_id(0) == 0)
    def _():
        copies = [
            pltpu.make_async_copy(g_hbm.at[0], g_ref, sems.at[0]),
            pltpu.make_async_copy(u_hbm.at[0], u_ref, sems.at[1]),
            pltpu.make_async_copy(d_hbm, d_ref, sems.at[2]),
        ]
        for c in copies:
            c.start()
        out_ref[...] = ffn_rows(x_ref[...], g_ref, u_ref, d_ref, copies)

    @pl.when(pl.program_id(0) > 0)
    def _():
        out_ref[...] = ffn_rows(x_ref[...], g_ref, u_ref, d_ref)


def part_kernel(x_ref, g_ref, u_ref, d_ref, into_ref, out_ref):
    out_ref[...] = ffn_rows(x_ref[...], g_ref, u_ref, d_ref)


def ffn_part(first, count, x, g, u, d_t, into=None):
    hbm, vm = pl.BlockSpec(memory_space=pltpu.HBM), pl.BlockSpec(memory_space=pltpu.VMEM)
    block = pl.BlockSpec((384, 2880), lambda i: (first + i, 0))
    start = into is None
    held = [pltpu.VMEM((2880, 768), BF)] * 3
    return pl.pallas_call(
        first_kernel if start else part_kernel,
        grid=(count,),
        in_specs=[block] + ([hbm] * 3 if start else [vm] * 3 + [hbm]),
        out_specs=[block] + [vm] * 3 * start,
        out_shape=[pltpu.HBM((1536, 2880), BF)] + held * start,
        scratch_shapes=[pltpu.SemaphoreType.DMA((3,))] * start,
        input_output_aliases={} if start else {4: 0},
        compiler_params=pltpu.CompilerParams(vmem_limit_bytes=(41 if start else 30) << 20),
        cost_estimate=pl.CostEstimate(
            flops=6 * 384 * count * 2880 * 768, bytes_accessed=4_500_000 * count, transcendentals=384 * 768 * count
        ),
        name="ffn_part%d" % first,
    )(x, g, u, d_t, *([] if start else [into]))


def combine_kernel(at_ref, y_ref, own_tail_ref, sib_tail_ref, own_ref, sib_ref, w_ref, acc_ref):
    step = pl.program_id(0)

    @pl.when(step == 0)
    def _():
        for side, ref in enumerate((own_tail_ref, sib_tail_ref)):
            w = row_weights(ref[...], at_ref[0], side, True).T.astype(BF)
            for b in range(6):
                w_ref[b, 128 * side : 128 * side + 128, :] = w[:, 128 * b : 128 * b + 128]
        acc_ref[...] = jnp.zeros_like(acc_ref)

    w = w_ref[step]
    acc_ref[...] += jnp.dot(w, y_ref[0], preferred_element_type=F32) + jnp.dot(
        w, y_ref[1], preferred_element_type=F32
    )

    @pl.when(step == 5)
    def _():
        own_ref[...] = acc_ref[:128, :].T
        sib_ref[...] = acc_ref[128:, :].T.astype(BF)


def combine(at, y, own_tail, sib_tail):
    vm = pl.BlockSpec(memory_space=pltpu.VMEM)
    return pl.pallas_call(
        combine_kernel,
        grid=(6,),
        in_specs=[
            pl.BlockSpec(memory_space=pltpu.SMEM),
            pl.BlockSpec((2, 128, 2880), lambda i: (0, i, 0)),
            vm,
            vm,
        ],
        out_specs=[pl.BlockSpec((2880, 128), lambda i: (0, 0))] * 2,
        out_shape=[jax.ShapeDtypeStruct((2880, 128), F32), jax.ShapeDtypeStruct((2880, 128), BF)],
        scratch_shapes=[pltpu.VMEM((6, 256, 128), BF), pltpu.VMEM((256, 2880), F32)],
        compiler_params=pltpu.CompilerParams(vmem_limit_bytes=48 << 20),
        cost_estimate=pl.CostEstimate(flops=4 * 768 * 256 * 2880, bytes_accessed=12_000_000, transcendentals=0),
        name="combine",
    )(at, y, own_tail, sib_tail)


def grad_kernel(at_ref, p0_ref, p1_ref, p2_ref, p3_ref, mine_ref, far_ref, out_ref):
    y, x = at_ref[1], at_ref[3]
    total = None
    for o, (one, two) in ((0, (p0_ref, p1_ref)), (2, (p2_ref, p3_ref))):
        right = [
            jnp.concatenate([mine_ref[(y + o + i) & 3], far_ref[(y + o + i) & 3]], axis=1) for i in range(2)
        ]
        left = jnp.concatenate([one[...], two[...]], axis=1)
        term = jnp.dot(left, jnp.concatenate(right, axis=0), preferred_element_type=F32)
        total = term if total is None else total + term
    for j in range(4):
        for side in range(2):
            low = 512 * side + 128 * j
            out_ref[0, pl.ds((j - x) & 3, 1), 0, side] = total[None, :, low : low + 128].astype(BF)


def local_grad(at, blocks, mine, far):
    vm = pl.BlockSpec(memory_space=pltpu.VMEM)
    return pl.pallas_call(
        grad_kernel,
        grid_spec=pltpu.PrefetchScalarGridSpec(
            num_scalar_prefetch=1,
            grid=(4,),
            in_specs=[pl.BlockSpec((720, 128), lambda i, at: (i, 0))] * 4 + [vm, vm],
            out_specs=pl.BlockSpec(
                (1, 4, 1, 2, 720, 128), lambda i, at: ((i >> 1) ^ at[0], 0, (i & 1) ^ at[4], 0, 0, 0)
            ),
        ),
        out_shape=jax.ShapeDtypeStruct((2, 4, 2, 2, 720, 128), BF),
        compiler_params=pltpu.CompilerParams(vmem_limit_bytes=32 << 20),
        cost_estimate=pl.CostEstimate(flops=2 * 1024 * 512 * 2880, bytes_accessed=10_000_000, transcendentals=0),
        name="local_grad",
    )(at, *blocks, mine, far)


def sum_kernel(a_ref, b_ref, c_ref, d_ref, kept_ref, gone_ref):
    total = a_ref[...] + b_ref[...].astype(F32) + c_ref[...].astype(F32) + d_ref[...].astype(F32)
    kept_ref[...] = total[0]
    gone_ref[...] = total[1].astype(BF)


def sum_terms(own, terms):
    vm = pl.BlockSpec(memory_space=pltpu.VMEM)
    return pl.pallas_call(
        sum_kernel,
        in_specs=[vm] * 4,
        out_specs=[vm] * 2,
        out_shape=[jax.ShapeDtypeStruct((2, 720, 128), F32), jax.ShapeDtypeStruct((2, 720, 128), BF)],
        compiler_params=pltpu.CompilerParams(vmem_limit_bytes=16 << 20),
        cost_estimate=pl.CostEstimate(flops=1 << 20, bytes_accessed=4_800_000, transcendentals=0),
        name="sum_terms",
    )(own, *terms)


def spread_kernel(at_ref, own_ref, sib_ref, out_ref):
    core = at_ref[0]
    out_ref[pl.ds(core, 1)] = own_ref[...].astype(F32)
    out_ref[pl.ds(1 - core, 1)] = sib_ref[...].astype(F32)


def spread(at, own, sib):
    block = pl.BlockSpec((1, 1440, 128), lambda i, at: (i, 0, 0))
    return pl.pallas_call(
        spread_kernel,
        grid_spec=pltpu.PrefetchScalarGridSpec(
            num_scalar_prefetch=1,
            grid=(4,),
            in_specs=[block, block],
            out_specs=pl.BlockSpec((2, 1440, 128), lambda i, at: (0, 0, (at[3] + i) & 3)),
        ),
        out_shape=jax.ShapeDtypeStruct((2, 1440, 512), F32),
        compiler_params=pltpu.CompilerParams(vmem_limit_bytes=16 << 20),
        cost_estimate=pl.CostEstimate(flops=0, bytes_accessed=9_000_000, transcendentals=0),
        name="spread",
    )(at, own, sib)


def shift(axis, by, n):
    return functools.partial(lax.ppermute, axis_name=axis, perm=[(i, (i + by) % n) for i in range(n)])


def from_others(block, axis):
    return [shift(axis, -o, 4)(block) for o in (1, 2, 3)]


def after(value, *others):
    return lax.optimization_barrier((value,) + others)[0]


def local(tokens, expert_ids, gate_raw, overflow_shift, limits, gate_w, up_w, down_w, context, out_grad):
    at = jnp.stack([lax.axis_index(a) for a in ("core", "y", "zl", "x", "zh")]).astype(jnp.int32)
    zh, zl = lax.axis_index("zh"), lax.axis_index("zl")
    core_swap, zl_swap, zh_swap = shift("core", 1, 2), shift("zl", 1, 2), shift("zh", 1, 2)
    over = ("zl", "x", "zh", "y")

    def exchange(rows):
        return lax.all_to_all(rows.reshape(64, 24, 2880), over, split_axis=0, concat_axis=0, tiled=True)

    og = out_grad.T
    ogs = from_others(og, "y")
    ctx = context.reshape(4, 2, 128, 512)
    ctx_mine = lax.dynamic_index_in_dim(ctx, zl, 1, keepdims=False)
    ctx_far = zl_swap(lax.dynamic_index_in_dim(ctx, 1 - zl, 1, keepdims=False))

    lim = jnp.broadcast_to(limits.astype(F32)[:, None], (64, 128))
    mine = place_call(tokens.T, expert_ids.T, overflow_shift.T, gate_raw.T, lim)
    sibling = core_swap(mine)
    got = exchange(after(rows_of(at, mine, sibling), ctx_far, *ogs)).reshape(1536, 2880)

    grads = local_grad(at, [og] + ogs, ctx_mine, ctx_far)
    part = grads[0].astype(F32) + core_swap(grads[1]).astype(F32)
    terms = [shift("x", o, 4)(part[o].astype(BF)) for o in (1, 2, 3)]
    out, *weights = ffn_part(0, 1, after(got, part), gate_w, up_w, down_w[0].T)
    terms = lax.optimization_barrier((*terms, out))[:-1]
    kept, gone = sum_terms(part[0], terms)
    came = zh_swap(gone)
    (out,) = ffn_part(1, 1, got, *weights, after(out, gone))
    total = kept + after(came, out).astype(F32)
    gone = total[1].astype(BF)
    came = zl_swap(gone)
    (out,) = ffn_part(2, 1, got, *weights, after(out, gone))
    final = (total[0] + after(came, out).astype(F32)).astype(BF)
    back = zh_swap(final)
    (out,) = ffn_part(3, 1, got, *weights, after(out, final))
    back = after(back, out)
    block = jnp.concatenate([jnp.where(zh == 0, final, back), jnp.where(zh == 0, back, final)])
    full = jnp.stack([block] + from_others(block, "x"))
    grad = spread(at, full, core_swap(full)).reshape(2880, 512)

    out = exchange(after(out, block))
    own, sib = combine(at, out.reshape(2, 768, 2880), mine[2880:], sibling[2880:])
    mixed = (own + core_swap(sib).astype(F32)).astype(BF)
    return mixed.T, grad.T


def solution(mesh):
    fine = Mesh(mesh.devices.reshape(4, 2, 2, 4, 2), ("x", "zh", "core", "y", "zl"))
    every = ("x", "zh", "core", "y", "zl")
    two, three = P(every, None), P(every, None, None)
    in_specs = (two, two, two, two, P(), three, three, three, P(("x", "zh", "core"), ("y", "zl")), two)
    out_specs = (two, P(("y", "zl"), None))
    return jax.shard_map(local, mesh=fine, in_specs=in_specs, out_specs=out_specs, check_vma=False)
```

```python
import functools

import jax
import jax.numpy as jnp
from jax import lax
from jax.experimental import pallas as pl
from jax.experimental.pallas import tpu as pltpu
from jax.sharding import Mesh, PartitionSpec as P

CAP = 12
BF = jnp.bfloat16
F32 = jnp.float32
NT = (((1,), (1,)), ((), ()))


def place(ids, shifts, lim):
    label = lax.broadcasted_iota(jnp.int32, (64, 128), 0)
    earlier = (
        lax.broadcasted_iota(jnp.int32, (128, 128), 0)
        < lax.broadcasted_iota(jnp.int32, (128, 128), 1)
    ).astype(F32).astype(BF)
    rows = [ids[k : k + 1, :] for k in range(4)]
    hots = [(r == label).astype(F32) for r in rows]
    hot = hots[0] + hots[1] + hots[2] + hots[3]
    before = jnp.dot(hot.astype(BF), earlier, preferred_element_type=F32)
    spilled, seconds, second_hots, first_ranks = [], [], [], []
    for k in range(4):
        rank = jnp.sum(before * hots[k], axis=0, keepdims=True)
        limit = jnp.sum(lim * hots[k], axis=0, keepdims=True)
        spill = rank >= limit
        second = (rows[k] + shifts[k : k + 1, :]) & 63
        first_ranks.append(rank)
        spilled.append(spill)
        seconds.append(second)
        second_hots.append((second == label).astype(F32))
    spill_hots = [h * s.astype(F32) for h, s in zip(second_hots, spilled)]
    total = spill_hots[0] + spill_hots[1] + spill_hots[2] + spill_hots[3]
    run = jnp.dot(total.astype(BF), earlier, preferred_element_type=F32)
    out = []
    for k in range(4):
        rank = jnp.sum(run * second_hots[k], axis=0, keepdims=True)
        run = run + spill_hots[k]
        limit = jnp.sum(lim * second_hots[k], axis=0, keepdims=True)
        slot = jnp.where(spilled[k], limit + rank, first_ranks[k]).astype(jnp.int32)
        target = jnp.where(spilled[k], seconds[k], rows[k])
        out.append((target, slot, slot < CAP))
    return out


def place_kernel(tok_ref, ids_ref, shift_ref, raw_ref, lim_ref, out_ref):
    out_ref[:2880, :] = tok_ref[...]
    places = place(ids_ref[...], shift_ref[...], lim_ref[...])
    raw = raw_ref[...]
    share = raw / jnp.sum(raw, axis=0, keepdims=True)
    rows = [t.astype(F32) for t, _, _ in places]
    rows += [jnp.where(k, s, -1).astype(F32) for _, s, k in places]
    rows += [share, jnp.zeros((4, 128), F32)]
    out_ref[2880:, :] = jnp.concatenate(rows, axis=0).astype(BF)


def place_call(tok, ids, shifts, raw, lim):
    vm = pl.BlockSpec(memory_space=pltpu.VMEM)
    return pl.pallas_call(
        place_kernel,
        in_specs=[vm] * 5,
        out_specs=vm,
        out_shape=jax.ShapeDtypeStruct((2896, 128), BF),
        compiler_params=pltpu.CompilerParams(vmem_limit_bytes=16 << 20),
        cost_estimate=pl.CostEstimate(flops=1 << 22, bytes_accessed=1_500_000, transcendentals=0),
        name="place",
    )(tok, ids, shifts, raw, lim)


def row_hot(tail, core, y, side):
    tail = tail.astype(F32)
    at = lax.broadcasted_iota(jnp.int32, (192, 128), 0)
    hot = None
    for k in range(4):
        target = tail[k : k + 1].astype(jnp.int32)
        slot = tail[4 + k : 5 + k].astype(jnp.int32)
        mine = (slot >= 0) & (((target >> 2) & 1) == core) & ((target & 3) == y)
        one = jnp.where(mine, (target >> 3) * 24 + side * CAP + slot, -1) == at
        hot = one if hot is None else hot | one
    return hot.astype(F32).astype(BF)


def picked_rows(own_ref, sib_ref, core, y):
    hot = jnp.concatenate(
        [row_hot(own_ref[2880:, :], core, y, 0), row_hot(sib_ref[2880:, :], core, y, 1)], axis=1
    )
    both = jnp.concatenate([own_ref[:2880, :], sib_ref[:2880, :]], axis=1)
    return lax.dot_general(hot, both, NT, preferred_element_type=F32)


def near_kernel(at_ref, own_ref, sib_ref, out_ref):
    got = picked_rows(own_ref, sib_ref, at_ref[0], at_ref[1]).astype(BF)
    out_ref[0] = got
    out_ref[1] = got


def near_rows(at, own, sib):
    vm = pl.BlockSpec(memory_space=pltpu.VMEM)
    return pl.pallas_call(
        near_kernel,
        in_specs=[pl.BlockSpec(memory_space=pltpu.SMEM), vm, vm],
        out_specs=vm,
        out_shape=jax.ShapeDtypeStruct((2, 192, 2880), BF),
        compiler_params=pltpu.CompilerParams(vmem_limit_bytes=24 << 20),
        cost_estimate=pl.CostEstimate(flops=2 * 192 * 256 * 2880, bytes_accessed=3_700_000, transcendentals=0),
        name="near_rows",
    )(at, own, sib)


def far_kernel(at_ref, *refs):
    out_ref = refs[6]
    for o in range(3):

        @pl.when(pl.program_id(0) == o)
        def _(o=o):
            got = picked_rows(refs[2 * o], refs[2 * o + 1], at_ref[0], at_ref[1])
            got = got.reshape(8, 24, 2880).astype(BF)
            out_ref[0, :, 0] = got
            out_ref[1, :, 0] = got


def far_rows(at, blocks):
    vm = pl.BlockSpec(memory_space=pltpu.VMEM)
    return pl.pallas_call(
        far_kernel,
        grid=(3,),
        in_specs=[pl.BlockSpec(memory_space=pltpu.SMEM)] + [vm] * 6,
        out_specs=pl.BlockSpec((2, 8, 1, 24, 2880), lambda i: (0, 0, i, 0, 0)),
        out_shape=jax.ShapeDtypeStruct((2, 8, 3, 24, 2880), BF),
        compiler_params=pltpu.CompilerParams(vmem_limit_bytes=48 << 20),
        cost_estimate=pl.CostEstimate(flops=6 * 192 * 256 * 2880, bytes_accessed=11_000_000, transcendentals=0),
        name="far_rows",
    )(at, *blocks)


def ffn_rows(x, g_ref, u_ref, d_ref, copies=(None,) * 3):
    def ready(i):
        if copies[i] is not None:
            copies[i].wait()

    ready(0)
    gating = jnp.dot(x, g_ref[...], preferred_element_type=F32)
    ready(1)
    upward = jnp.dot(x, u_ref[...], preferred_element_type=F32)
    active = ((upward + 1.0) * gating * jax.nn.sigmoid(1.702 * gating)).astype(BF)
    ready(2)
    return lax.dot_general(active, d_ref[...], NT, preferred_element_type=F32)


def started(g_hbm, u_hbm, d_hbm, g_ref, u_ref, d_ref, sems):
    copies = [
        pltpu.make_async_copy(g_hbm.at[0], g_ref, sems.at[0]),
        pltpu.make_async_copy(u_hbm.at[0], u_ref, sems.at[1]),
        pltpu.make_async_copy(d_hbm, d_ref, sems.at[2]),
    ]
    for c in copies:
        c.start()
    return copies


def near_ffn_kernel(at_ref, x_ref, g_hbm, u_hbm, d_hbm, out_ref, g_ref, u_ref, d_ref, sems):
    copies = started(g_hbm, u_hbm, d_hbm, g_ref, u_ref, d_ref, sems)
    got = ffn_rows(x_ref[...], g_ref, u_ref, d_ref, copies)
    out_ref[:, 0] = got.reshape(16, 24, 2880).astype(BF)


def first_kernel(at_ref, x_ref, g_hbm, u_hbm, d_hbm, into_ref, out_ref, g_ref, u_ref, d_ref, sems):
    copies = started(g_hbm, u_hbm, d_hbm, g_ref, u_ref, d_ref, sems)
    got = ffn_rows(x_ref[:, 0].reshape(384, 2880), g_ref, u_ref, d_ref, copies)
    out_ref[:, 0] = got.reshape(16, 24, 2880).astype(BF)


def part_kernel(at_ref, x_ref, g_ref, u_ref, d_ref, into_ref, out_ref):
    got = ffn_rows(x_ref[:, 0].reshape(384, 2880), g_ref, u_ref, d_ref)
    out_ref[:, 0] = got.reshape(16, 24, 2880).astype(BF)


def ffn_part(at, o, x, g, u, d_t, into=None):
    hbm, vm = pl.BlockSpec(memory_space=pltpu.HBM), pl.BlockSpec(memory_space=pltpu.VMEM)
    kernel = (near_ffn_kernel, first_kernel, part_kernel, part_kernel)[o]
    held = [pltpu.VMEM((2880, 768), BF)] * 3
    sems = [pltpu.SemaphoreType.DMA((3,))]
    if o == 0:
        x_spec = pl.BlockSpec((384, 2880), lambda i, at: (0, 0))
    else:
        x_spec = pl.BlockSpec((16, 1, 24, 2880), lambda i, at: (0, o - 1, 0, 0))
    return pl.pallas_call(
        kernel,
        grid_spec=pltpu.PrefetchScalarGridSpec(
            num_scalar_prefetch=1,
            grid=(1,),
            in_specs=[x_spec] + [vm if o > 1 else hbm] * 3 + [hbm] * (o > 0),
            out_specs=[pl.BlockSpec((16, 1, 24, 2880), lambda i, at: (0, (at[1] + o) & 3, 0, 0))]
            + [vm] * 3 * (o == 1),
            scratch_shapes=(held + sems, sems, [], [])[o],
        ),
        out_shape=[pltpu.HBM((16, 4, 24, 2880), BF)] + held * (o == 1),
        input_output_aliases={5: 0} if o else {},
        compiler_params=pltpu.CompilerParams(vmem_limit_bytes=(60, 47, 30, 30)[o] << 20),
        cost_estimate=pl.CostEstimate(
            flops=6 * 384 * 2880 * 768, bytes_accessed=18_000_000, transcendentals=384 * 768
        ),
        name="ffn_part%d" % o,
    )(at, x, g, u, d_t, *([into] if o else []))


def combine_kernel(at_ref, y_ref, own_tail_ref, sib_tail_ref, ahead_ref, own_ref, sib_ref, w_ref, acc_ref):
    step = pl.program_id(0)

    @pl.when(step == 0)
    def _():
        core = at_ref[0]
        slot_of = lax.broadcasted_iota(jnp.int32, (768, 128), 0)
        for side, ref in enumerate((own_tail_ref, sib_tail_ref)):
            tail = ref[...].astype(F32)
            w = jnp.zeros((768, 128), F32)
            for k in range(4):
                target = tail[k : k + 1].astype(jnp.int32)
                slot = tail[4 + k : 5 + k].astype(jnp.int32)
                mine = (slot >= 0) & (((target >> 2) & 1) == core)
                row = jnp.where(mine, ((target >> 3) * 4 + (target & 3)) * 24 + side * CAP + slot, -1)
                w = w + jnp.where(row == slot_of, tail[8 + k : 9 + k], 0.0)
            wt = w.T.astype(BF)
            for b in range(4):
                w_ref[b, 128 * side : 128 * side + 128, :] = wt[:, 192 * b : 192 * b + 192]
        acc_ref[...] = jnp.zeros_like(acc_ref)

    w = w_ref[step]
    acc_ref[...] += jnp.dot(w, y_ref[0], preferred_element_type=F32) + jnp.dot(
        w, y_ref[1], preferred_element_type=F32
    )

    @pl.when(step == 3)
    def _():
        own_ref[...] = acc_ref[:128, :].T
        sib_ref[...] = acc_ref[128:, :].T.astype(BF)


def combine(at, y, own_tail, sib_tail, ahead):
    vm = pl.BlockSpec(memory_space=pltpu.VMEM)
    return pl.pallas_call(
        combine_kernel,
        grid=(4,),
        in_specs=[
            pl.BlockSpec(memory_space=pltpu.SMEM),
            pl.BlockSpec((2, 192, 2880), lambda i: (0, i, 0)),
            vm,
            vm,
            pl.BlockSpec(memory_space=pl.ANY),
        ],
        out_specs=[pl.BlockSpec((2880, 128), lambda i: (0, 0))] * 2,
        out_shape=[jax.ShapeDtypeStruct((2880, 128), F32), jax.ShapeDtypeStruct((2880, 128), BF)],
        scratch_shapes=[pltpu.VMEM((4, 256, 192), BF), pltpu.VMEM((256, 2880), F32)],
        compiler_params=pltpu.CompilerParams(vmem_limit_bytes=48 << 20),
        cost_estimate=pl.CostEstimate(flops=4 * 768 * 256 * 2880, bytes_accessed=12_000_000, transcendentals=0),
        name="combine",
    )(at, y, own_tail, sib_tail, ahead)


def grad_kernel(at_ref, p0_ref, p1_ref, p2_ref, p3_ref, ctx_ref, out_ref):
    y, zl, x = at_ref[1], at_ref[2], at_ref[3]
    total = None
    for o, ref in enumerate((p0_ref, p1_ref, p2_ref, p3_ref)):
        base = ((y + o) & 3) * 256
        same = ctx_ref[pl.ds(pl.multiple_of(base + zl * 128, 128), 128), :]
        other = ctx_ref[pl.ds(pl.multiple_of(base + (1 - zl) * 128, 128), 128), :]
        left = jnp.concatenate([ref[0], ref[1]], axis=1)
        term = jnp.dot(left, jnp.concatenate([same, other], axis=0), preferred_element_type=F32)
        total = term if total is None else total + term
    for j in range(4):
        out_ref[0, 0, pl.ds((j - x) & 3, 1)] = total[None, :, 128 * j : 128 * j + 128].astype(BF)


def local_grad(at, pairs, context):
    return pl.pallas_call(
        grad_kernel,
        grid_spec=pltpu.PrefetchScalarGridSpec(
            num_scalar_prefetch=1,
            grid=(4,),
            in_specs=[pl.BlockSpec((2, 720, 128), lambda i, at: (0, i, 0))] * 4
            + [pl.BlockSpec(memory_space=pltpu.VMEM)],
            out_specs=pl.BlockSpec((1, 1, 4, 720, 128), lambda i, at: ((i >> 1) ^ at[0], (i & 1) ^ at[4], 0, 0, 0)),
        ),
        out_shape=jax.ShapeDtypeStruct((2, 2, 4, 720, 128), BF),
        compiler_params=pltpu.CompilerParams(vmem_limit_bytes=24 << 20),
        cost_estimate=pl.CostEstimate(flops=2 * 1024 * 512 * 2880, bytes_accessed=10_000_000, transcendentals=0),
        name="local_grad",
    )(at, *pairs, context)


def spread_kernel(at_ref, own_ref, sib_ref, out_ref):
    core, zh = at_ref[0], at_ref[4]
    for c, ref in ((core, own_ref), (1 - core, sib_ref)):
        for k, z in ((0, zh), (1, 1 - zh)):
            out_ref[pl.ds(c, 1), pl.ds(z, 1)] = ref[k : k + 1].astype(F32)


def spread(at, own, sib):
    block = pl.BlockSpec((2, 1, 720, 128), lambda i, at: (0, i, 0, 0))
    return pl.pallas_call(
        spread_kernel,
        grid_spec=pltpu.PrefetchScalarGridSpec(
            num_scalar_prefetch=1,
            grid=(4,),
            in_specs=[block, block],
            out_specs=pl.BlockSpec((2, 2, 720, 128), lambda i, at: (0, 0, 0, (at[3] + i) & 3)),
        ),
        out_shape=jax.ShapeDtypeStruct((2, 2, 720, 512), F32),
        compiler_params=pltpu.CompilerParams(vmem_limit_bytes=16 << 20),
        cost_estimate=pl.CostEstimate(flops=0, bytes_accessed=9_000_000, transcendentals=0),
        name="spread",
    )(at, own, sib)


def shift(axis, by, n):
    return functools.partial(lax.ppermute, axis_name=axis, perm=[(i, (i + by) % n) for i in range(n)])


def from_others(block, axis):
    return [shift(axis, -o, 4)(block) for o in (1, 2, 3)]


def after(value, *others):
    return lax.optimization_barrier((value,) + others)[0]


def local(tokens, expert_ids, gate_raw, overflow_shift, limits, gate_w, up_w, down_w, context, out_grad):
    at = jnp.stack([lax.axis_index(a) for a in ("core", "y", "zl", "x", "zh")]).astype(jnp.int32)
    core_swap, zl_swap, zh_swap = shift("core", 1, 2), shift("zl", 1, 2), shift("zh", 1, 2)
    over = ("zl", "x", "zh")

    lim = jnp.broadcast_to(limits.astype(F32)[:, None], (64, 128))
    mine = place_call(tokens.T, expert_ids.T, overflow_shift.T, gate_raw.T, lim)
    og = out_grad.T
    og_other = zl_swap(og)
    sibling = core_swap(mine)
    others = from_others(mine, "y")
    near = near_rows(at, mine, sibling).reshape(16, 24, 2880)
    near = lax.all_to_all(near, over, split_axis=0, concat_axis=0, tiled=True)
    blocks = []
    for block in others:
        blocks += [block, core_swap(block)]
    pair = jnp.stack([og, og_other])
    far = after(far_rows(at, blocks), og_other, near).reshape(16, 72, 2880)
    far = lax.all_to_all(far, over, split_axis=0, concat_axis=0, tiled=True)
    far = far.reshape(16, 3, 24, 2880)

    hbm_weights = gate_w, up_w, down_w[0].T
    (out,) = ffn_part(at, 0, near.reshape(384, 2880), *hbm_weights)
    pairs = [after(pair, out)] + from_others(pair, "y")
    grads = local_grad(at, pairs, context)
    part = grads[0].astype(F32) + core_swap(grads[1]).astype(F32)
    part = part[0] + zh_swap(part[1].astype(BF)).astype(F32)
    sends = [part[o].astype(BF) for o in (1, 2, 3)]
    terms = [shift("x", o, 4)(block) for o, block in zip((1, 2, 3), sends)]
    out, *weights = ffn_part(at, 1, after(far, *sends), *hbm_weights, out)
    terms = lax.optimization_barrier((*terms, out))[:3]
    final = (part[0] + terms[0].astype(F32) + terms[1].astype(F32) + terms[2].astype(F32)).astype(BF)
    blocks = from_others(final, "x")
    (out,) = ffn_part(at, 2, far, *weights, after(out, final))
    blocks = lax.optimization_barrier((*blocks, out))[:3]
    half = jnp.stack([final, *blocks])
    opposite = zh_swap(half)
    full = jnp.stack([half, opposite])
    (out,) = ffn_part(at, 3, far, *weights, after(out, half))
    grad = spread(at, full, core_swap(full)).reshape(2880, 512)

    out = after(out, opposite).reshape(64, 24, 2880)
    out = lax.all_to_all(out, over + ("y",), split_axis=0, concat_axis=0, tiled=True)
    own, sib = combine(at, out.reshape(2, 768, 2880), mine[2880:], sibling[2880:], grad)
    mixed = (own + core_swap(sib).astype(F32)).astype(BF)
    return mixed.T, grad.T


def solution(mesh):
    fine = Mesh(mesh.devices.reshape(4, 2, 2, 4, 2), ("x", "zh", "core", "y", "zl"))
    every = ("x", "zh", "core", "y", "zl")
    two, three = P(every, None), P(every, None, None)
    in_specs = (two, two, two, two, P(), three, three, three, P(("x", "zh", "core"), ("y", "zl")), two)
    out_specs = (two, P(("y", "zl"), None))
    return jax.shard_map(local, mesh=fine, in_specs=in_specs, out_specs=out_specs, check_vma=False)
```

```python
import functools

import jax
import jax.numpy as jnp
from jax import lax
from jax.experimental import pallas as pl
from jax.experimental.pallas import tpu as pltpu
from jax.sharding import Mesh, PartitionSpec as P

CAP = 12
BF = jnp.bfloat16
F32 = jnp.float32
NT = (((1,), (1,)), ((), ()))


def place(ids, shifts, lim):
    label = lax.broadcasted_iota(jnp.int32, (64, 128), 0)
    earlier = (
        lax.broadcasted_iota(jnp.int32, (128, 128), 0)
        < lax.broadcasted_iota(jnp.int32, (128, 128), 1)
    ).astype(F32).astype(BF)
    rows = [ids[k : k + 1, :] for k in range(4)]
    hots = [(r == label).astype(F32) for r in rows]
    hot = hots[0] + hots[1] + hots[2] + hots[3]
    before = jnp.dot(hot.astype(BF), earlier, preferred_element_type=F32)
    spilled, seconds, second_hots, first_ranks = [], [], [], []
    for k in range(4):
        rank = jnp.sum(before * hots[k], axis=0, keepdims=True)
        limit = jnp.sum(lim * hots[k], axis=0, keepdims=True)
        spill = rank >= limit
        second = (rows[k] + shifts[k : k + 1, :]) & 63
        first_ranks.append(rank)
        spilled.append(spill)
        seconds.append(second)
        second_hots.append((second == label).astype(F32))
    spill_hots = [h * s.astype(F32) for h, s in zip(second_hots, spilled)]
    total = spill_hots[0] + spill_hots[1] + spill_hots[2] + spill_hots[3]
    run = jnp.dot(total.astype(BF), earlier, preferred_element_type=F32)
    out = []
    for k in range(4):
        rank = jnp.sum(run * second_hots[k], axis=0, keepdims=True)
        run = run + spill_hots[k]
        limit = jnp.sum(lim * second_hots[k], axis=0, keepdims=True)
        slot = jnp.where(spilled[k], limit + rank, first_ranks[k]).astype(jnp.int32)
        target = jnp.where(spilled[k], seconds[k], rows[k])
        out.append((target, slot, slot < CAP))
    return out


def place_kernel(tok_ref, ids_ref, shift_ref, raw_ref, lim_ref, out_ref):
    out_ref[:2880, :] = tok_ref[...]
    places = place(ids_ref[...], shift_ref[...], lim_ref[...])
    raw = raw_ref[...]
    share = raw / jnp.sum(raw, axis=0, keepdims=True)
    rows = [t.astype(F32) for t, _, _ in places]
    rows += [jnp.where(k, s, -1).astype(F32) for _, s, k in places]
    rows += [share, jnp.zeros((4, 128), F32)]
    out_ref[2880:, :] = jnp.concatenate(rows, axis=0).astype(BF)


def place_call(tok, ids, shifts, raw, lim):
    vm = pl.BlockSpec(memory_space=pltpu.VMEM)
    return pl.pallas_call(
        place_kernel,
        in_specs=[vm] * 5,
        out_specs=vm,
        out_shape=jax.ShapeDtypeStruct((2896, 128), BF),
        compiler_params=pltpu.CompilerParams(vmem_limit_bytes=16 << 20),
        cost_estimate=pl.CostEstimate(flops=1 << 22, bytes_accessed=1_500_000, transcendentals=0),
        name="place",
    )(tok, ids, shifts, raw, lim)


def row_hot(tail, core, y, side):
    tail = tail.astype(F32)
    at = lax.broadcasted_iota(jnp.int32, (192, 128), 0)
    hot = None
    for k in range(4):
        target = tail[k : k + 1].astype(jnp.int32)
        slot = tail[4 + k : 5 + k].astype(jnp.int32)
        mine = (slot >= 0) & (((target >> 2) & 1) == core) & ((target & 3) == y)
        one = jnp.where(mine, (target >> 3) * 24 + side * CAP + slot, -1) == at
        hot = one if hot is None else hot | one
    return hot.astype(F32).astype(BF)


def picked_rows(own_ref, sib_ref, core, y):
    hot = jnp.concatenate(
        [row_hot(own_ref[2880:, :], core, y, 0), row_hot(sib_ref[2880:, :], core, y, 1)], axis=1
    )
    both = jnp.concatenate([own_ref[:2880, :], sib_ref[:2880, :]], axis=1)
    return lax.dot_general(hot, both, NT, preferred_element_type=F32)


def near_kernel(at_ref, own_ref, sib_ref, out_ref):
    got = picked_rows(own_ref, sib_ref, at_ref[0], at_ref[1]).astype(BF)
    out_ref[0] = got
    out_ref[1] = got


def near_rows(at, own, sib):
    vm = pl.BlockSpec(memory_space=pltpu.VMEM)
    return pl.pallas_call(
        near_kernel,
        in_specs=[pl.BlockSpec(memory_space=pltpu.SMEM), vm, vm],
        out_specs=vm,
        out_shape=jax.ShapeDtypeStruct((2, 192, 2880), BF),
        compiler_params=pltpu.CompilerParams(vmem_limit_bytes=24 << 20),
        cost_estimate=pl.CostEstimate(flops=2 * 192 * 256 * 2880, bytes_accessed=3_700_000, transcendentals=0),
        name="near_rows",
    )(at, own, sib)


def far_kernel(at_ref, *refs):
    out_ref = refs[6]
    for o in range(3):

        @pl.when(pl.program_id(0) == o)
        def _(o=o):
            got = picked_rows(refs[2 * o], refs[2 * o + 1], at_ref[0], at_ref[1])
            got = got.reshape(8, 24, 2880).astype(BF)
            out_ref[0, :, 0] = got
            out_ref[1, :, 0] = got


def far_rows(at, blocks):
    vm = pl.BlockSpec(memory_space=pltpu.VMEM)
    return pl.pallas_call(
        far_kernel,
        grid=(3,),
        in_specs=[pl.BlockSpec(memory_space=pltpu.SMEM)] + [vm] * 6,
        out_specs=pl.BlockSpec((2, 8, 1, 24, 2880), lambda i: (0, 0, i, 0, 0)),
        out_shape=jax.ShapeDtypeStruct((2, 8, 3, 24, 2880), BF),
        compiler_params=pltpu.CompilerParams(vmem_limit_bytes=48 << 20),
        cost_estimate=pl.CostEstimate(flops=6 * 192 * 256 * 2880, bytes_accessed=11_000_000, transcendentals=0),
        name="far_rows",
    )(at, *blocks)


def ffn_rows(x, g_ref, u_ref, d_ref, copies=(None,) * 3):
    def ready(i):
        if copies[i] is not None:
            copies[i].wait()

    ready(0)
    gating = jnp.dot(x, g_ref[...], preferred_element_type=F32)
    ready(1)
    upward = jnp.dot(x, u_ref[...], preferred_element_type=F32)
    active = ((upward + 1.0) * gating * jax.nn.sigmoid(1.702 * gating)).astype(BF)
    ready(2)
    return lax.dot_general(active, d_ref[...], NT, preferred_element_type=F32)


def started(g_hbm, u_hbm, d_hbm, g_ref, u_ref, d_ref, sems):
    copies = [
        pltpu.make_async_copy(g_hbm.at[0], g_ref, sems.at[0]),
        pltpu.make_async_copy(u_hbm.at[0], u_ref, sems.at[1]),
        pltpu.make_async_copy(d_hbm, d_ref, sems.at[2]),
    ]
    for c in copies:
        c.start()
    return copies


def near_ffn_kernel(at_ref, x_ref, g_hbm, u_hbm, d_hbm, out_ref, g_ref, u_ref, d_ref, sems):
    copies = started(g_hbm, u_hbm, d_hbm, g_ref, u_ref, d_ref, sems)
    got = ffn_rows(x_ref[...], g_ref, u_ref, d_ref, copies)
    out_ref[:, 0] = got.reshape(16, 24, 2880).astype(BF)


def first_kernel(at_ref, x_ref, g_hbm, u_hbm, d_hbm, into_ref, out_ref, g_ref, u_ref, d_ref, sems):
    copies = started(g_hbm, u_hbm, d_hbm, g_ref, u_ref, d_ref, sems)
    got = ffn_rows(x_ref[:, 0].reshape(384, 2880), g_ref, u_ref, d_ref, copies)
    out_ref[:, 0] = got.reshape(16, 24, 2880).astype(BF)


def part_kernel(at_ref, x_ref, g_ref, u_ref, d_ref, into_ref, out_ref):
    got = ffn_rows(x_ref[:, 0].reshape(384, 2880), g_ref, u_ref, d_ref)
    out_ref[:, 0] = got.reshape(16, 24, 2880).astype(BF)


def ffn_part(at, o, x, g, u, d_t, into=None):
    hbm, vm = pl.BlockSpec(memory_space=pltpu.HBM), pl.BlockSpec(memory_space=pltpu.VMEM)
    kernel = (near_ffn_kernel, first_kernel, part_kernel)[o]
    held = [pltpu.VMEM((2880, 768), BF)] * 3
    sems = [pltpu.SemaphoreType.DMA((3,))]
    if o == 0:
        x_spec = pl.BlockSpec((384, 2880), lambda i, at: (0, 0))
    else:
        x_spec = pl.BlockSpec((16, 1, 24, 2880), lambda i, at: (0, o - 1 + i, 0, 0))
    return pl.pallas_call(
        kernel,
        grid_spec=pltpu.PrefetchScalarGridSpec(
            num_scalar_prefetch=1,
            grid=(2 if o == 2 else 1,),
            in_specs=[x_spec] + [vm if o > 1 else hbm] * 3 + [hbm] * (o > 0),
            out_specs=[pl.BlockSpec((16, 1, 24, 2880), lambda i, at: (0, (at[1] + o + i) & 3, 0, 0))]
            + [vm] * 3 * (o == 1),
            scratch_shapes=(held + sems, sems, [])[o],
        ),
        out_shape=[pltpu.HBM((16, 4, 24, 2880), BF)] + held * (o == 1),
        input_output_aliases={5: 0} if o else {},
        compiler_params=pltpu.CompilerParams(vmem_limit_bytes=(60, 47, 30)[o] << 20),
        cost_estimate=pl.CostEstimate(
            flops=6 * 384 * 2880 * 768, bytes_accessed=18_000_000, transcendentals=384 * 768
        ),
        name="ffn_part%d" % o,
    )(at, x, g, u, d_t, *([into] if o else []))


def combine_kernel(at_ref, y_ref, own_tail_ref, sib_tail_ref, ahead_ref, own_ref, sib_ref, w_ref, acc_ref):
    step = pl.program_id(0)

    @pl.when(step == 0)
    def _():
        core = at_ref[0]
        slot_of = lax.broadcasted_iota(jnp.int32, (768, 128), 0)
        for side, ref in enumerate((own_tail_ref, sib_tail_ref)):
            tail = ref[...].astype(F32)
            w = jnp.zeros((768, 128), F32)
            for k in range(4):
                target = tail[k : k + 1].astype(jnp.int32)
                slot = tail[4 + k : 5 + k].astype(jnp.int32)
                mine = (slot >= 0) & (((target >> 2) & 1) == core)
                row = jnp.where(mine, ((target >> 3) * 4 + (target & 3)) * 24 + side * CAP + slot, -1)
                w = w + jnp.where(row == slot_of, tail[8 + k : 9 + k], 0.0)
            wt = w.T.astype(BF)
            for b in range(4):
                w_ref[b, 128 * side : 128 * side + 128, :] = wt[:, 192 * b : 192 * b + 192]
        acc_ref[...] = jnp.zeros_like(acc_ref)

    w = w_ref[step]
    acc_ref[...] += jnp.dot(w, y_ref[0], preferred_element_type=F32) + jnp.dot(
        w, y_ref[1], preferred_element_type=F32
    )

    @pl.when(step == 3)
    def _():
        own_ref[...] = acc_ref[:128, :].T
        sib_ref[...] = acc_ref[128:, :].T.astype(BF)


def combine(at, y, own_tail, sib_tail, ahead):
    vm = pl.BlockSpec(memory_space=pltpu.VMEM)
    return pl.pallas_call(
        combine_kernel,
        grid=(4,),
        in_specs=[
            pl.BlockSpec(memory_space=pltpu.SMEM),
            pl.BlockSpec((2, 192, 2880), lambda i: (0, i, 0)),
            vm,
            vm,
            pl.BlockSpec(memory_space=pl.ANY),
        ],
        out_specs=[pl.BlockSpec((2880, 128), lambda i: (0, 0))] * 2,
        out_shape=[jax.ShapeDtypeStruct((2880, 128), F32), jax.ShapeDtypeStruct((2880, 128), BF)],
        scratch_shapes=[pltpu.VMEM((4, 256, 192), BF), pltpu.VMEM((256, 2880), F32)],
        compiler_params=pltpu.CompilerParams(vmem_limit_bytes=48 << 20),
        cost_estimate=pl.CostEstimate(flops=4 * 768 * 256 * 2880, bytes_accessed=12_000_000, transcendentals=0),
        name="combine",
    )(at, y, own_tail, sib_tail, ahead)


def grad_kernel(at_ref, p0_ref, p1_ref, p2_ref, p3_ref, ctx_ref, out_ref):
    y, zl, x = at_ref[1], at_ref[2], at_ref[3]
    total = None
    for o, ref in enumerate((p0_ref, p1_ref, p2_ref, p3_ref)):
        base = ((y + o) & 3) * 256
        same = ctx_ref[pl.ds(pl.multiple_of(base + zl * 128, 128), 128), :]
        other = ctx_ref[pl.ds(pl.multiple_of(base + (1 - zl) * 128, 128), 128), :]
        left = jnp.concatenate([ref[0], ref[1]], axis=1)
        term = jnp.dot(left, jnp.concatenate([same, other], axis=0), preferred_element_type=F32)
        total = term if total is None else total + term
    for j in range(4):
        out_ref[0, pl.ds((j - x) & 3, 1)] = total[None, :, 128 * j : 128 * j + 128].astype(BF)


def local_grad(at, pairs, context):
    return pl.pallas_call(
        grad_kernel,
        grid_spec=pltpu.PrefetchScalarGridSpec(
            num_scalar_prefetch=1,
            grid=(4,),
            in_specs=[pl.BlockSpec((2, 720, 128), lambda i, at: (0, i, 0))] * 4
            + [pl.BlockSpec(memory_space=pltpu.VMEM)],
            out_specs=pl.BlockSpec((1, 4, 720, 128), lambda i, at: ((i >> 1) ^ at[0], 0, i & 1, 0)),
        ),
        out_shape=jax.ShapeDtypeStruct((2, 4, 1440, 128), BF),
        compiler_params=pltpu.CompilerParams(vmem_limit_bytes=24 << 20),
        cost_estimate=pl.CostEstimate(flops=2 * 1024 * 512 * 2880, bytes_accessed=10_000_000, transcendentals=0),
        name="local_grad",
    )(at, *pairs, context)


def spread_kernel(at_ref, own_ref, sib_ref, out_ref):
    core = at_ref[0]
    out_ref[pl.ds(core, 1)] = own_ref[...].astype(F32)
    out_ref[pl.ds(1 - core, 1)] = sib_ref[...].astype(F32)


def spread(at, own, sib):
    block = pl.BlockSpec((1, 1440, 128), lambda i, at: (i, 0, 0))
    return pl.pallas_call(
        spread_kernel,
        grid_spec=pltpu.PrefetchScalarGridSpec(
            num_scalar_prefetch=1,
            grid=(4,),
            in_specs=[block, block],
            out_specs=pl.BlockSpec((2, 1440, 128), lambda i, at: (0, 0, i)),
        ),
        out_shape=jax.ShapeDtypeStruct((2, 1440, 512), F32),
        compiler_params=pltpu.CompilerParams(vmem_limit_bytes=16 << 20),
        cost_estimate=pl.CostEstimate(flops=0, bytes_accessed=9_000_000, transcendentals=0),
        name="spread",
    )(at, own, sib)


def shift(axis, by, n):
    return functools.partial(lax.ppermute, axis_name=axis, perm=[(i, (i + by) % n) for i in range(n)])


def from_others(block, axis):
    return [shift(axis, -o, 4)(block) for o in (1, 2, 3)]


def after(value, *others):
    return lax.optimization_barrier((value,) + others)[0]


def local(tokens, expert_ids, gate_raw, overflow_shift, limits, gate_w, up_w, down_w, context, out_grad):
    at = jnp.stack([lax.axis_index(a) for a in ("core", "y", "zl", "x", "zh")]).astype(jnp.int32)
    zh = lax.axis_index("zh")
    core_swap, zl_swap, zh_swap = shift("core", 1, 2), shift("zl", 1, 2), shift("zh", 1, 2)
    over = ("zl", "x", "zh")

    lim = jnp.broadcast_to(limits.astype(F32)[:, None], (64, 128))
    mine = place_call(tokens.T, expert_ids.T, overflow_shift.T, gate_raw.T, lim)
    og = out_grad.T
    og_other = zl_swap(og)
    sibling = core_swap(mine)
    others = from_others(mine, "y")
    near = after(near_rows(at, mine, sibling), og_other, others[0], others[2]).reshape(16, 24, 2880)
    near = lax.all_to_all(near, over, split_axis=0, concat_axis=0, tiled=True)
    blocks = []
    for block in others:
        blocks += [block, core_swap(block)]
    pair = jnp.stack([og, og_other])
    far = after(far_rows(at, blocks), pair, near).reshape(16, 72, 2880)
    far = lax.all_to_all(far, over, split_axis=0, concat_axis=0, tiled=True)
    far = far.reshape(16, 3, 24, 2880)

    hbm_weights = gate_w, up_w, down_w[0].T
    (out,) = ffn_part(at, 0, near.reshape(384, 2880), *hbm_weights)
    pairs = [after(pair, out)] + from_others(pair, "y")
    grads = local_grad(at, pairs, context)
    part = grads[0].astype(F32) + core_swap(grads[1]).astype(F32)
    terms = [shift("x", o, 4)(part[o].astype(BF)) for o in (1, 2, 3)]
    out, *weights = ffn_part(at, 1, far, *hbm_weights, out)
    terms = lax.optimization_barrier((*terms, out))[:3]
    total = part[0] + terms[0].astype(F32) + terms[1].astype(F32) + terms[2].astype(F32)
    rows = total.reshape(2, 720, 128)
    kept = lax.dynamic_index_in_dim(rows, zh, 0, keepdims=False)
    gone = lax.dynamic_index_in_dim(rows, 1 - zh, 0, keepdims=False).astype(BF)
    came = zh_swap(gone)
    (out,) = ffn_part(at, 2, far, *weights, after(out, gone))
    total = (kept + after(came, out).astype(F32)).astype(BF)
    full = lax.all_gather(after(total, out), ("x", "zh"), axis=0, tiled=True).reshape(4, 1440, 128)
    grad = spread(at, full, core_swap(full)).reshape(2880, 512)

    out = after(out, total).reshape(64, 24, 2880)
    out = lax.all_to_all(out, over + ("y",), split_axis=0, concat_axis=0, tiled=True)
    own, sib = combine(at, out.reshape(2, 768, 2880), mine[2880:], sibling[2880:], grad)
    mixed = (own + core_swap(sib).astype(F32)).astype(BF)
    return mixed.T, grad.T


def solution(mesh):
    fine = Mesh(mesh.devices.reshape(4, 2, 2, 4, 2), ("x", "zh", "core", "y", "zl"))
    every = ("x", "zh", "core", "y", "zl")
    two, three = P(every, None), P(every, None, None)
    in_specs = (two, two, two, two, P(), three, three, three, P(("x", "zh", "core"), ("y", "zl")), two)
    out_specs = (two, P(("y", "zl"), None))
    return jax.shard_map(local, mesh=fine, in_specs=in_specs, out_specs=out_specs, check_vma=False)
```

```python
import functools

import jax
import jax.numpy as jnp
from jax import lax
from jax.experimental import pallas as pl
from jax.experimental.pallas import tpu as pltpu
from jax.sharding import Mesh, PartitionSpec as P

CAP = 12
BF = jnp.bfloat16
F32 = jnp.float32
NT = (((1,), (1,)), ((), ()))


def place(ids, shifts, lim):
    label = lax.broadcasted_iota(jnp.int32, (64, 128), 0)
    earlier = (
        lax.broadcasted_iota(jnp.int32, (128, 128), 0)
        < lax.broadcasted_iota(jnp.int32, (128, 128), 1)
    ).astype(F32).astype(BF)
    rows = [ids[k : k + 1, :] for k in range(4)]
    hots = [(r == label).astype(F32) for r in rows]
    hot = hots[0] + hots[1] + hots[2] + hots[3]
    before = jnp.dot(hot.astype(BF), earlier, preferred_element_type=F32)
    spilled, seconds, second_hots, first_ranks = [], [], [], []
    for k in range(4):
        rank = jnp.sum(before * hots[k], axis=0, keepdims=True)
        limit = jnp.sum(lim * hots[k], axis=0, keepdims=True)
        spill = rank >= limit
        second = (rows[k] + shifts[k : k + 1, :]) & 63
        first_ranks.append(rank)
        spilled.append(spill)
        seconds.append(second)
        second_hots.append((second == label).astype(F32))
    spill_hots = [h * s.astype(F32) for h, s in zip(second_hots, spilled)]
    total = spill_hots[0] + spill_hots[1] + spill_hots[2] + spill_hots[3]
    run = jnp.dot(total.astype(BF), earlier, preferred_element_type=F32)
    out = []
    for k in range(4):
        rank = jnp.sum(run * second_hots[k], axis=0, keepdims=True)
        run = run + spill_hots[k]
        limit = jnp.sum(lim * second_hots[k], axis=0, keepdims=True)
        slot = jnp.where(spilled[k], limit + rank, first_ranks[k]).astype(jnp.int32)
        target = jnp.where(spilled[k], seconds[k], rows[k])
        out.append((target, slot, slot < CAP))
    return out


def place_kernel(tok_ref, ids_ref, shift_ref, raw_ref, lim_ref, out_ref):
    out_ref[:2880, :] = tok_ref[...]
    places = place(ids_ref[...], shift_ref[...], lim_ref[...])
    raw = raw_ref[...]
    share = raw / jnp.sum(raw, axis=0, keepdims=True)
    rows = [t.astype(F32) for t, _, _ in places]
    rows += [jnp.where(k, s, -1).astype(F32) for _, s, k in places]
    rows += [share, jnp.zeros((4, 128), F32)]
    out_ref[2880:, :] = jnp.concatenate(rows, axis=0).astype(BF)


def place_call(tok, ids, shifts, raw, lim):
    vm = pl.BlockSpec(memory_space=pltpu.VMEM)
    return pl.pallas_call(
        place_kernel,
        in_specs=[vm] * 5,
        out_specs=vm,
        out_shape=jax.ShapeDtypeStruct((2896, 128), BF),
        compiler_params=pltpu.CompilerParams(vmem_limit_bytes=16 << 20),
        cost_estimate=pl.CostEstimate(flops=1 << 22, bytes_accessed=1_500_000, transcendentals=0),
        name="place",
    )(tok, ids, shifts, raw, lim)


def row_hot(tail, core, y, side):
    tail = tail.astype(F32)
    at = lax.broadcasted_iota(jnp.int32, (192, 128), 0)
    hot = None
    for k in range(4):
        target = tail[k : k + 1].astype(jnp.int32)
        slot = tail[4 + k : 5 + k].astype(jnp.int32)
        mine = (slot >= 0) & (((target >> 2) & 1) == core) & ((target & 3) == y)
        one = jnp.where(mine, (target >> 3) * 24 + side * CAP + slot, -1) == at
        hot = one if hot is None else hot | one
    return hot.astype(F32).astype(BF)


def picked_rows(own_ref, sib_ref, core, y):
    hot = jnp.concatenate(
        [row_hot(own_ref[2880:, :], core, y, 0), row_hot(sib_ref[2880:, :], core, y, 1)], axis=1
    )
    both = jnp.concatenate([own_ref[:2880, :], sib_ref[:2880, :]], axis=1)
    return lax.dot_general(hot, both, NT, preferred_element_type=F32)


def near_kernel(at_ref, own_ref, sib_ref, out_ref):
    got = picked_rows(own_ref, sib_ref, at_ref[0], at_ref[1]).astype(BF)
    out_ref[0] = got
    out_ref[1] = got


def near_rows(at, own, sib):
    vm = pl.BlockSpec(memory_space=pltpu.VMEM)
    return pl.pallas_call(
        near_kernel,
        in_specs=[pl.BlockSpec(memory_space=pltpu.SMEM), vm, vm],
        out_specs=vm,
        out_shape=jax.ShapeDtypeStruct((2, 192, 2880), BF),
        compiler_params=pltpu.CompilerParams(vmem_limit_bytes=24 << 20),
        cost_estimate=pl.CostEstimate(flops=2 * 192 * 256 * 2880, bytes_accessed=3_700_000, transcendentals=0),
        name="near_rows",
    )(at, own, sib)


def far_kernel(at_ref, *refs):
    out_ref = refs[6]
    for o in range(3):

        @pl.when(pl.program_id(0) == o)
        def _(o=o):
            got = picked_rows(refs[2 * o], refs[2 * o + 1], at_ref[0], at_ref[1])
            got = got.reshape(8, 24, 2880).astype(BF)
            out_ref[0, :, 0] = got
            out_ref[1, :, 0] = got


def far_rows(at, blocks):
    vm = pl.BlockSpec(memory_space=pltpu.VMEM)
    return pl.pallas_call(
        far_kernel,
        grid=(3,),
        in_specs=[pl.BlockSpec(memory_space=pltpu.SMEM)] + [vm] * 6,
        out_specs=pl.BlockSpec((2, 8, 1, 24, 2880), lambda i: (0, 0, i, 0, 0)),
        out_shape=jax.ShapeDtypeStruct((2, 8, 3, 24, 2880), BF),
        compiler_params=pltpu.CompilerParams(vmem_limit_bytes=48 << 20),
        cost_estimate=pl.CostEstimate(flops=6 * 192 * 256 * 2880, bytes_accessed=11_000_000, transcendentals=0),
        name="far_rows",
    )(at, *blocks)


def ffn_rows(x, g_ref, u_ref, d_ref, copies=(None,) * 3):
    def ready(i):
        if copies[i] is not None:
            copies[i].wait()

    ready(0)
    gating = jnp.dot(x, g_ref[...], preferred_element_type=F32)
    ready(1)
    upward = jnp.dot(x, u_ref[...], preferred_element_type=F32)
    active = ((upward + 1.0) * gating * jax.nn.sigmoid(1.702 * gating)).astype(BF)
    ready(2)
    return lax.dot_general(active, d_ref[...], NT, preferred_element_type=F32)


def started(g_hbm, u_hbm, d_hbm, g_ref, u_ref, d_ref, sems):
    copies = [
        pltpu.make_async_copy(g_hbm.at[0], g_ref, sems.at[0]),
        pltpu.make_async_copy(u_hbm.at[0], u_ref, sems.at[1]),
        pltpu.make_async_copy(d_hbm, d_ref, sems.at[2]),
    ]
    for c in copies:
        c.start()
    return copies


def near_ffn_kernel(at_ref, x_ref, g_hbm, u_hbm, d_hbm, out_ref, g_ref, u_ref, d_ref, sems):
    copies = started(g_hbm, u_hbm, d_hbm, g_ref, u_ref, d_ref, sems)
    got = ffn_rows(x_ref[...], g_ref, u_ref, d_ref, copies)
    out_ref[:, 0] = got.reshape(16, 24, 2880).astype(BF)


def first_kernel(at_ref, x_ref, g_hbm, u_hbm, d_hbm, into_ref, out_ref, g_ref, u_ref, d_ref, sems):
    copies = started(g_hbm, u_hbm, d_hbm, g_ref, u_ref, d_ref, sems)
    got = ffn_rows(x_ref[:, 0].reshape(384, 2880), g_ref, u_ref, d_ref, copies)
    out_ref[:, 0] = got.reshape(16, 24, 2880).astype(BF)


def part_kernel(at_ref, x_ref, g_ref, u_ref, d_ref, into_ref, out_ref):
    got = ffn_rows(x_ref[:, 0].reshape(384, 2880), g_ref, u_ref, d_ref)
    out_ref[:, 0] = got.reshape(16, 24, 2880).astype(BF)


def ffn_part(at, o, x, g, u, d_t, into=None):
    hbm, vm = pl.BlockSpec(memory_space=pltpu.HBM), pl.BlockSpec(memory_space=pltpu.VMEM)
    kernel = (near_ffn_kernel, first_kernel, part_kernel, part_kernel)[o]
    held = [pltpu.VMEM((2880, 768), BF)] * 3
    sems = [pltpu.SemaphoreType.DMA((3,))]
    if o == 0:
        x_spec = pl.BlockSpec((384, 2880), lambda i, at: (0, 0))
    else:
        x_spec = pl.BlockSpec((16, 1, 24, 2880), lambda i, at: (0, o - 1, 0, 0))
    return pl.pallas_call(
        kernel,
        grid_spec=pltpu.PrefetchScalarGridSpec(
            num_scalar_prefetch=1,
            grid=(1,),
            in_specs=[x_spec] + [vm if o > 1 else hbm] * 3 + [hbm] * (o > 0),
            out_specs=[pl.BlockSpec((16, 1, 24, 2880), lambda i, at: (0, (at[1] + o) & 3, 0, 0))]
            + [vm] * 3 * (o == 1),
            scratch_shapes=(held + sems, sems, [], [])[o],
        ),
        out_shape=[pltpu.HBM((16, 4, 24, 2880), BF)] + held * (o == 1),
        input_output_aliases={5: 0} if o else {},
        compiler_params=pltpu.CompilerParams(vmem_limit_bytes=(60, 47, 30, 30)[o] << 20),
        cost_estimate=pl.CostEstimate(
            flops=6 * 384 * 2880 * 768, bytes_accessed=18_000_000, transcendentals=384 * 768
        ),
        name="ffn_part%d" % o,
    )(at, x, g, u, d_t, *([into] if o else []))


def combine_kernel(at_ref, y_ref, own_tail_ref, sib_tail_ref, ahead_ref, own_ref, sib_ref, w_ref, acc_ref):
    step = pl.program_id(0)

    @pl.when(step == 0)
    def _():
        core = at_ref[0]
        slot_of = lax.broadcasted_iota(jnp.int32, (768, 128), 0)
        for side, ref in enumerate((own_tail_ref, sib_tail_ref)):
            tail = ref[...].astype(F32)
            w = jnp.zeros((768, 128), F32)
            for k in range(4):
                target = tail[k : k + 1].astype(jnp.int32)
                slot = tail[4 + k : 5 + k].astype(jnp.int32)
                mine = (slot >= 0) & (((target >> 2) & 1) == core)
                row = jnp.where(mine, ((target >> 3) * 4 + (target & 3)) * 24 + side * CAP + slot, -1)
                w = w + jnp.where(row == slot_of, tail[8 + k : 9 + k], 0.0)
            wt = w.T.astype(BF)
            for b in range(4):
                w_ref[b, 128 * side : 128 * side + 128, :] = wt[:, 192 * b : 192 * b + 192]
        acc_ref[...] = jnp.zeros_like(acc_ref)

    w = w_ref[step]
    acc_ref[...] += jnp.dot(w, y_ref[0], preferred_element_type=F32) + jnp.dot(
        w, y_ref[1], preferred_element_type=F32
    )

    @pl.when(step == 3)
    def _():
        own_ref[...] = acc_ref[:128, :].T
        sib_ref[...] = acc_ref[128:, :].T.astype(BF)


def combine(at, y, own_tail, sib_tail, ahead):
    vm = pl.BlockSpec(memory_space=pltpu.VMEM)
    return pl.pallas_call(
        combine_kernel,
        grid=(4,),
        in_specs=[
            pl.BlockSpec(memory_space=pltpu.SMEM),
            pl.BlockSpec((2, 192, 2880), lambda i: (0, i, 0)),
            vm,
            vm,
            pl.BlockSpec(memory_space=pl.ANY),
        ],
        out_specs=[pl.BlockSpec((2880, 128), lambda i: (0, 0))] * 2,
        out_shape=[jax.ShapeDtypeStruct((2880, 128), F32), jax.ShapeDtypeStruct((2880, 128), BF)],
        scratch_shapes=[pltpu.VMEM((4, 256, 192), BF), pltpu.VMEM((256, 2880), F32)],
        compiler_params=pltpu.CompilerParams(vmem_limit_bytes=48 << 20),
        cost_estimate=pl.CostEstimate(flops=4 * 768 * 256 * 2880, bytes_accessed=12_000_000, transcendentals=0),
        name="combine",
    )(at, y, own_tail, sib_tail, ahead)


def grad_kernel(at_ref, p0_ref, p1_ref, p2_ref, p3_ref, ctx_ref, out_ref):
    y, zl, x = at_ref[1], at_ref[2], at_ref[3]
    total = None
    for o, ref in enumerate((p0_ref, p1_ref, p2_ref, p3_ref)):
        base = ((y + o) & 3) * 256
        same = ctx_ref[pl.ds(pl.multiple_of(base + zl * 128, 128), 128), :]
        other = ctx_ref[pl.ds(pl.multiple_of(base + (1 - zl) * 128, 128), 128), :]
        left = jnp.concatenate([ref[0], ref[1]], axis=1)
        term = jnp.dot(left, jnp.concatenate([same, other], axis=0), preferred_element_type=F32)
        total = term if total is None else total + term
    for j in range(4):
        out_ref[0, pl.ds((j - x) & 3, 1)] = total[None, :, 128 * j : 128 * j + 128].astype(BF)


def local_grad(at, pairs, context):
    return pl.pallas_call(
        grad_kernel,
        grid_spec=pltpu.PrefetchScalarGridSpec(
            num_scalar_prefetch=1,
            grid=(4,),
            in_specs=[pl.BlockSpec((2, 720, 128), lambda i, at: (0, i, 0))] * 4
            + [pl.BlockSpec(memory_space=pltpu.VMEM)],
            out_specs=pl.BlockSpec((1, 4, 720, 128), lambda i, at: ((i >> 1) ^ at[0], 0, i & 1, 0)),
        ),
        out_shape=jax.ShapeDtypeStruct((2, 4, 1440, 128), BF),
        compiler_params=pltpu.CompilerParams(vmem_limit_bytes=24 << 20),
        cost_estimate=pl.CostEstimate(flops=2 * 1024 * 512 * 2880, bytes_accessed=10_000_000, transcendentals=0),
        name="local_grad",
    )(at, *pairs, context)


def spread_kernel(at_ref, own_ref, sib_ref, out_ref):
    core = at_ref[0]
    out_ref[pl.ds(core, 1)] = own_ref[...].astype(F32)
    out_ref[pl.ds(1 - core, 1)] = sib_ref[...].astype(F32)


def spread(at, own, sib):
    block = pl.BlockSpec((1, 1440, 128), lambda i, at: (i, 0, 0))
    return pl.pallas_call(
        spread_kernel,
        grid_spec=pltpu.PrefetchScalarGridSpec(
            num_scalar_prefetch=1,
            grid=(4,),
            in_specs=[block, block],
            out_specs=pl.BlockSpec((2, 1440, 128), lambda i, at: (0, 0, (at[3] + i) & 3)),
        ),
        out_shape=jax.ShapeDtypeStruct((2, 1440, 512), F32),
        compiler_params=pltpu.CompilerParams(vmem_limit_bytes=16 << 20),
        cost_estimate=pl.CostEstimate(flops=0, bytes_accessed=9_000_000, transcendentals=0),
        name="spread",
    )(at, own, sib)


def shift(axis, by, n):
    return functools.partial(lax.ppermute, axis_name=axis, perm=[(i, (i + by) % n) for i in range(n)])


def from_others(block, axis):
    return [shift(axis, -o, 4)(block) for o in (1, 2, 3)]


def after(value, *others):
    return lax.optimization_barrier((value,) + others)[0]


def local(tokens, expert_ids, gate_raw, overflow_shift, limits, gate_w, up_w, down_w, context, out_grad):
    at = jnp.stack([lax.axis_index(a) for a in ("core", "y", "zl", "x", "zh")]).astype(jnp.int32)
    zh = lax.axis_index("zh")
    core_swap, zl_swap, zh_swap = shift("core", 1, 2), shift("zl", 1, 2), shift("zh", 1, 2)
    over = ("zl", "x", "zh")

    lim = jnp.broadcast_to(limits.astype(F32)[:, None], (64, 128))
    mine = place_call(tokens.T, expert_ids.T, overflow_shift.T, gate_raw.T, lim)
    og = out_grad.T
    og_other = zl_swap(og)
    sibling = core_swap(mine)
    others = from_others(mine, "y")
    near = after(near_rows(at, mine, sibling), og_other, others[0], others[2]).reshape(16, 24, 2880)
    near = lax.all_to_all(near, over, split_axis=0, concat_axis=0, tiled=True)
    blocks = []
    for block in others:
        blocks += [block, core_swap(block)]
    pair = jnp.stack([og, og_other])
    far = after(far_rows(at, blocks), pair, near).reshape(16, 72, 2880)
    far = lax.all_to_all(far, over, split_axis=0, concat_axis=0, tiled=True)
    far = far.reshape(16, 3, 24, 2880)

    hbm_weights = gate_w, up_w, down_w[0].T
    (out,) = ffn_part(at, 0, near.reshape(384, 2880), *hbm_weights)
    pairs = [after(pair, out)] + from_others(pair, "y")
    grads = local_grad(at, pairs, context)
    part = grads[0].astype(F32) + core_swap(grads[1]).astype(F32)
    terms = [shift("x", o, 4)(part[o].astype(BF)) for o in (1, 2, 3)]
    out, *weights = ffn_part(at, 1, far, *hbm_weights, out)
    terms = lax.optimization_barrier((*terms, out))[:3]
    total = part[0] + terms[0].astype(F32) + terms[1].astype(F32) + terms[2].astype(F32)
    rows = total.reshape(2, 720, 128)
    kept = lax.dynamic_index_in_dim(rows, zh, 0, keepdims=False)
    gone = lax.dynamic_index_in_dim(rows, 1 - zh, 0, keepdims=False).astype(BF)
    came = zh_swap(gone)
    (out,) = ffn_part(at, 2, far, *weights, after(out, gone))
    total = (kept + after(came, out).astype(F32)).astype(BF)
    back = zh_swap(total)
    (out,) = ffn_part(at, 3, far, *weights, after(out, total))
    back = after(back, out)
    block = jnp.concatenate([jnp.where(zh == 0, total, back), jnp.where(zh == 0, back, total)])
    blocks = from_others(block, "x")
    full = jnp.stack([block] + blocks)
    grad = spread(at, full, core_swap(full)).reshape(2880, 512)

    out = after(out, *blocks).reshape(64, 24, 2880)
    out = lax.all_to_all(out, over + ("y",), split_axis=0, concat_axis=0, tiled=True)
    own, sib = combine(at, out.reshape(2, 768, 2880), mine[2880:], sibling[2880:], grad)
    mixed = (own + core_swap(sib).astype(F32)).astype(BF)
    return mixed.T, grad.T


def solution(mesh):
    fine = Mesh(mesh.devices.reshape(4, 2, 2, 4, 2), ("x", "zh", "core", "y", "zl"))
    every = ("x", "zh", "core", "y", "zl")
    two, three = P(every, None), P(every, None, None)
    in_specs = (two, two, two, two, P(), three, three, three, P(("x", "zh", "core"), ("y", "zl")), two)
    out_specs = (two, P(("y", "zl"), None))
    return jax.shard_map(local, mesh=fine, in_specs=in_specs, out_specs=out_specs, check_vma=False)
```

```python
import functools

import jax
import jax.numpy as jnp
from jax import lax
from jax.experimental import pallas as pl
from jax.experimental.pallas import tpu as pltpu
from jax.sharding import Mesh, PartitionSpec as P

CAP = 12
BF = jnp.bfloat16
F32 = jnp.float32
NT = (((1,), (1,)), ((), ()))


def place(ids, shifts, lim):
    label = lax.broadcasted_iota(jnp.int32, (64, 128), 0)
    earlier = (
        lax.broadcasted_iota(jnp.int32, (128, 128), 0)
        < lax.broadcasted_iota(jnp.int32, (128, 128), 1)
    ).astype(F32).astype(BF)
    rows = [ids[k : k + 1, :] for k in range(4)]
    hots = [(r == label).astype(F32) for r in rows]
    hot = hots[0] + hots[1] + hots[2] + hots[3]
    before = jnp.dot(hot.astype(BF), earlier, preferred_element_type=F32)
    spilled, seconds, second_hots, first_ranks = [], [], [], []
    for k in range(4):
        rank = jnp.sum(before * hots[k], axis=0, keepdims=True)
        limit = jnp.sum(lim * hots[k], axis=0, keepdims=True)
        spill = rank >= limit
        second = (rows[k] + shifts[k : k + 1, :]) & 63
        first_ranks.append(rank)
        spilled.append(spill)
        seconds.append(second)
        second_hots.append((second == label).astype(F32))
    spill_hots = [h * s.astype(F32) for h, s in zip(second_hots, spilled)]
    total = spill_hots[0] + spill_hots[1] + spill_hots[2] + spill_hots[3]
    run = jnp.dot(total.astype(BF), earlier, preferred_element_type=F32)
    out = []
    for k in range(4):
        rank = jnp.sum(run * second_hots[k], axis=0, keepdims=True)
        run = run + spill_hots[k]
        limit = jnp.sum(lim * second_hots[k], axis=0, keepdims=True)
        slot = jnp.where(spilled[k], limit + rank, first_ranks[k]).astype(jnp.int32)
        target = jnp.where(spilled[k], seconds[k], rows[k])
        out.append((target, slot, slot < CAP))
    return out


def place_kernel(tok_ref, ids_ref, shift_ref, raw_ref, lim_ref, out_ref):
    out_ref[:2880, :] = tok_ref[...]
    places = place(ids_ref[...], shift_ref[...], lim_ref[...])
    raw = raw_ref[...]
    share = raw / jnp.sum(raw, axis=0, keepdims=True)
    rows = [t.astype(F32) for t, _, _ in places]
    rows += [jnp.where(k, s, -1).astype(F32) for _, s, k in places]
    rows += [share, jnp.zeros((4, 128), F32)]
    out_ref[2880:, :] = jnp.concatenate(rows, axis=0).astype(BF)


def place_call(tok, ids, shifts, raw, lim):
    vm = pl.BlockSpec(memory_space=pltpu.VMEM)
    return pl.pallas_call(
        place_kernel,
        in_specs=[vm] * 5,
        out_specs=vm,
        out_shape=jax.ShapeDtypeStruct((2896, 128), BF),
        compiler_params=pltpu.CompilerParams(vmem_limit_bytes=16 << 20),
        cost_estimate=pl.CostEstimate(flops=1 << 22, bytes_accessed=1_500_000, transcendentals=0),
        name="place",
    )(tok, ids, shifts, raw, lim)


def row_hot(tail, core, y, side):
    tail = tail.astype(F32)
    at = lax.broadcasted_iota(jnp.int32, (192, 128), 0)
    hot = None
    for k in range(4):
        target = tail[k : k + 1].astype(jnp.int32)
        slot = tail[4 + k : 5 + k].astype(jnp.int32)
        mine = (slot >= 0) & (((target >> 2) & 1) == core) & ((target & 3) == y)
        one = jnp.where(mine, (target >> 3) * 24 + side * CAP + slot, -1) == at
        hot = one if hot is None else hot | one
    return hot.astype(F32).astype(BF)


def picked_rows(own_ref, sib_ref, core, y):
    hot = jnp.concatenate(
        [row_hot(own_ref[2880:, :], core, y, 0), row_hot(sib_ref[2880:, :], core, y, 1)], axis=1
    )
    both = jnp.concatenate([own_ref[:2880, :], sib_ref[:2880, :]], axis=1)
    return lax.dot_general(hot, both, NT, preferred_element_type=F32)


def near_kernel(at_ref, own_ref, sib_ref, out_ref):
    got = picked_rows(own_ref, sib_ref, at_ref[0], at_ref[1]).astype(BF)
    out_ref[0] = got
    out_ref[1] = got


def near_rows(at, own, sib):
    vm = pl.BlockSpec(memory_space=pltpu.VMEM)
    return pl.pallas_call(
        near_kernel,
        in_specs=[pl.BlockSpec(memory_space=pltpu.SMEM), vm, vm],
        out_specs=vm,
        out_shape=jax.ShapeDtypeStruct((2, 192, 2880), BF),
        compiler_params=pltpu.CompilerParams(vmem_limit_bytes=24 << 20),
        cost_estimate=pl.CostEstimate(flops=2 * 192 * 256 * 2880, bytes_accessed=3_700_000, transcendentals=0),
        name="near_rows",
    )(at, own, sib)


def far_kernel(at_ref, *refs):
    out_ref = refs[6]
    for o in range(3):

        @pl.when(pl.program_id(0) == o)
        def _(o=o):
            got = picked_rows(refs[2 * o], refs[2 * o + 1], at_ref[0], at_ref[1])
            got = got.reshape(8, 24, 2880).astype(BF)
            out_ref[0, :, 0] = got
            out_ref[1, :, 0] = got


def far_rows(at, blocks):
    vm = pl.BlockSpec(memory_space=pltpu.VMEM)
    return pl.pallas_call(
        far_kernel,
        grid=(3,),
        in_specs=[pl.BlockSpec(memory_space=pltpu.SMEM)] + [vm] * 6,
        out_specs=pl.BlockSpec((2, 8, 1, 24, 2880), lambda i: (0, 0, i, 0, 0)),
        out_shape=jax.ShapeDtypeStruct((2, 8, 3, 24, 2880), BF),
        compiler_params=pltpu.CompilerParams(vmem_limit_bytes=48 << 20),
        cost_estimate=pl.CostEstimate(flops=6 * 192 * 256 * 2880, bytes_accessed=11_000_000, transcendentals=0),
        name="far_rows",
    )(at, *blocks)


def ffn_rows(x, g_ref, u_ref, d_ref, copies=(None,) * 3):
    def ready(i):
        if copies[i] is not None:
            copies[i].wait()

    ready(0)
    gating = jnp.dot(x, g_ref[...], preferred_element_type=F32)
    ready(1)
    upward = jnp.dot(x, u_ref[...], preferred_element_type=F32)
    active = ((upward + 1.0) * gating * jax.nn.sigmoid(1.702 * gating)).astype(BF)
    ready(2)
    return lax.dot_general(active, d_ref[...], NT, preferred_element_type=F32)


def started(g_hbm, u_hbm, d_hbm, g_ref, u_ref, d_ref, sems):
    copies = [
        pltpu.make_async_copy(g_hbm.at[0], g_ref, sems.at[0]),
        pltpu.make_async_copy(u_hbm.at[0], u_ref, sems.at[1]),
        pltpu.make_async_copy(d_hbm, d_ref, sems.at[2]),
    ]
    for c in copies:
        c.start()
    return copies


def near_ffn_kernel(at_ref, x_ref, g_hbm, u_hbm, d_hbm, out_ref, g_ref, u_ref, d_ref, sems):
    copies = started(g_hbm, u_hbm, d_hbm, g_ref, u_ref, d_ref, sems)
    got = ffn_rows(x_ref[...], g_ref, u_ref, d_ref, copies)
    out_ref[:, 0] = got.reshape(16, 24, 2880).astype(BF)


def first_kernel(at_ref, x_ref, g_hbm, u_hbm, d_hbm, into_ref, out_ref, g_ref, u_ref, d_ref, sems):
    copies = started(g_hbm, u_hbm, d_hbm, g_ref, u_ref, d_ref, sems)
    got = ffn_rows(x_ref[:, 0].reshape(384, 2880), g_ref, u_ref, d_ref, copies)
    out_ref[:, 0] = got.reshape(16, 24, 2880).astype(BF)


def part_kernel(at_ref, x_ref, g_ref, u_ref, d_ref, into_ref, out_ref):
    got = ffn_rows(x_ref[:, 0].reshape(384, 2880), g_ref, u_ref, d_ref)
    out_ref[:, 0] = got.reshape(16, 24, 2880).astype(BF)


def ffn_part(at, o, x, g, u, d_t, into=None):
    hbm, vm = pl.BlockSpec(memory_space=pltpu.HBM), pl.BlockSpec(memory_space=pltpu.VMEM)
    kernel = (near_ffn_kernel, first_kernel, part_kernel)[o]
    held = [pltpu.VMEM((2880, 768), BF)] * 3
    sems = [pltpu.SemaphoreType.DMA((3,))]
    if o == 0:
        x_spec = pl.BlockSpec((384, 2880), lambda i, at: (0, 0))
    else:
        x_spec = pl.BlockSpec((16, 1, 24, 2880), lambda i, at: (0, o - 1 + i, 0, 0))
    return pl.pallas_call(
        kernel,
        grid_spec=pltpu.PrefetchScalarGridSpec(
            num_scalar_prefetch=1,
            grid=(2 if o == 2 else 1,),
            in_specs=[x_spec] + [vm if o > 1 else hbm] * 3 + [hbm] * (o > 0),
            out_specs=[pl.BlockSpec((16, 1, 24, 2880), lambda i, at: (0, (at[1] + o + i) & 3, 0, 0))]
            + [vm] * 3 * (o == 1),
            scratch_shapes=(held + sems, sems, [])[o],
        ),
        out_shape=[pltpu.HBM((16, 4, 24, 2880), BF)] + held * (o == 1),
        input_output_aliases={5: 0} if o else {},
        compiler_params=pltpu.CompilerParams(vmem_limit_bytes=(60, 47, 30)[o] << 20),
        cost_estimate=pl.CostEstimate(
            flops=6 * 384 * 2880 * 768, bytes_accessed=18_000_000, transcendentals=384 * 768
        ),
        name="ffn_part%d" % o,
    )(at, x, g, u, d_t, *([into] if o else []))


def combine_kernel(at_ref, y_ref, own_tail_ref, sib_tail_ref, ahead_ref, own_ref, sib_ref, w_ref, acc_ref):
    step = pl.program_id(0)

    @pl.when(step == 0)
    def _():
        core = at_ref[0]
        slot_of = lax.broadcasted_iota(jnp.int32, (768, 128), 0)
        for side, ref in enumerate((own_tail_ref, sib_tail_ref)):
            tail = ref[...].astype(F32)
            w = jnp.zeros((768, 128), F32)
            for k in range(4):
                target = tail[k : k + 1].astype(jnp.int32)
                slot = tail[4 + k : 5 + k].astype(jnp.int32)
                mine = (slot >= 0) & (((target >> 2) & 1) == core)
                row = jnp.where(mine, ((target >> 3) * 4 + (target & 3)) * 24 + side * CAP + slot, -1)
                w = w + jnp.where(row == slot_of, tail[8 + k : 9 + k], 0.0)
            wt = w.T.astype(BF)
            for b in range(4):
                w_ref[b, 128 * side : 128 * side + 128, :] = wt[:, 192 * b : 192 * b + 192]
        acc_ref[...] = jnp.zeros_like(acc_ref)

    w = w_ref[step]
    acc_ref[...] += jnp.dot(w, y_ref[0], preferred_element_type=F32) + jnp.dot(
        w, y_ref[1], preferred_element_type=F32
    )

    @pl.when(step == 3)
    def _():
        own_ref[...] = acc_ref[:128, :].T
        sib_ref[...] = acc_ref[128:, :].T.astype(BF)


def combine(at, y, own_tail, sib_tail, ahead):
    vm = pl.BlockSpec(memory_space=pltpu.VMEM)
    return pl.pallas_call(
        combine_kernel,
        grid=(4,),
        in_specs=[
            pl.BlockSpec(memory_space=pltpu.SMEM),
            pl.BlockSpec((2, 192, 2880), lambda i: (0, i, 0)),
            vm,
            vm,
            pl.BlockSpec(memory_space=pl.ANY),
        ],
        out_specs=[pl.BlockSpec((2880, 128), lambda i: (0, 0))] * 2,
        out_shape=[jax.ShapeDtypeStruct((2880, 128), F32), jax.ShapeDtypeStruct((2880, 128), BF)],
        scratch_shapes=[pltpu.VMEM((4, 256, 192), BF), pltpu.VMEM((256, 2880), F32)],
        compiler_params=pltpu.CompilerParams(vmem_limit_bytes=48 << 20),
        cost_estimate=pl.CostEstimate(flops=4 * 768 * 256 * 2880, bytes_accessed=12_000_000, transcendentals=0),
        name="combine",
    )(at, y, own_tail, sib_tail, ahead)


def grad_kernel(at_ref, p0_ref, p1_ref, p2_ref, p3_ref, ctx_ref, out_ref):
    y, zl, x = at_ref[1], at_ref[2], at_ref[3]
    total = None
    for o, ref in enumerate((p0_ref, p1_ref, p2_ref, p3_ref)):
        base = ((y + o) & 3) * 256
        same = ctx_ref[pl.ds(pl.multiple_of(base + zl * 128, 128), 128), :]
        other = ctx_ref[pl.ds(pl.multiple_of(base + (1 - zl) * 128, 128), 128), :]
        left = jnp.concatenate([ref[0], ref[1]], axis=1)
        term = jnp.dot(left, jnp.concatenate([same, other], axis=0), preferred_element_type=F32)
        total = term if total is None else total + term
    for j in range(4):
        out_ref[0, pl.ds((j - x) & 3, 1)] = total[None, :, 128 * j : 128 * j + 128].astype(BF)


def local_grad(at, pairs, context):
    return pl.pallas_call(
        grad_kernel,
        grid_spec=pltpu.PrefetchScalarGridSpec(
            num_scalar_prefetch=1,
            grid=(4,),
            in_specs=[pl.BlockSpec((2, 720, 128), lambda i, at: (0, i, 0))] * 4
            + [pl.BlockSpec(memory_space=pltpu.VMEM)],
            out_specs=pl.BlockSpec((1, 4, 720, 128), lambda i, at: ((i >> 1) ^ at[0], 0, i & 1, 0)),
        ),
        out_shape=jax.ShapeDtypeStruct((2, 4, 1440, 128), BF),
        compiler_params=pltpu.CompilerParams(vmem_limit_bytes=24 << 20),
        cost_estimate=pl.CostEstimate(flops=2 * 1024 * 512 * 2880, bytes_accessed=10_000_000, transcendentals=0),
        name="local_grad",
    )(at, *pairs, context)


def spread_kernel(at_ref, own_ref, sib_ref, out_ref):
    core = at_ref[0]
    out_ref[pl.ds(core, 1)] = own_ref[...].astype(F32)
    out_ref[pl.ds(1 - core, 1)] = sib_ref[...].astype(F32)


def spread(at, own, sib):
    block = pl.BlockSpec((1, 1440, 128), lambda i, at: (i, 0, 0))
    return pl.pallas_call(
        spread_kernel,
        grid_spec=pltpu.PrefetchScalarGridSpec(
            num_scalar_prefetch=1,
            grid=(4,),
            in_specs=[block, block],
            out_specs=pl.BlockSpec((2, 1440, 128), lambda i, at: (0, 0, i)),
        ),
        out_shape=jax.ShapeDtypeStruct((2, 1440, 512), F32),
        compiler_params=pltpu.CompilerParams(vmem_limit_bytes=16 << 20),
        cost_estimate=pl.CostEstimate(flops=0, bytes_accessed=9_000_000, transcendentals=0),
        name="spread",
    )(at, own, sib)


def shift(axis, by, n):
    return functools.partial(lax.ppermute, axis_name=axis, perm=[(i, (i + by) % n) for i in range(n)])


def from_others(block, axis):
    return [shift(axis, -o, 4)(block) for o in (1, 2, 3)]


def after(value, *others):
    return lax.optimization_barrier((value,) + others)[0]


def local(tokens, expert_ids, gate_raw, overflow_shift, limits, gate_w, up_w, down_w, context, out_grad):
    at = jnp.stack([lax.axis_index(a) for a in ("core", "y", "zl", "x", "zh")]).astype(jnp.int32)
    zh = lax.axis_index("zh")
    core_swap, zl_swap, zh_swap = shift("core", 1, 2), shift("zl", 1, 2), shift("zh", 1, 2)
    over = ("zl", "x", "zh")

    lim = jnp.broadcast_to(limits.astype(F32)[:, None], (64, 128))
    mine = place_call(tokens.T, expert_ids.T, overflow_shift.T, gate_raw.T, lim)
    og = out_grad.T
    og_other = zl_swap(og)
    sibling = core_swap(mine)
    others = from_others(mine, "y")
    near = after(near_rows(at, mine, sibling), og_other, others[0], others[2]).reshape(16, 24, 2880)
    near = lax.all_to_all(near, over, split_axis=0, concat_axis=0, tiled=True)
    blocks = []
    for block in others:
        blocks += [block, core_swap(block)]
    pair = jnp.stack([og, og_other])
    far = after(far_rows(at, blocks), pair, near).reshape(16, 72, 2880)
    far = lax.all_to_all(far, over, split_axis=0, concat_axis=0, tiled=True)
    far = far.reshape(16, 3, 24, 2880)

    hbm_weights = gate_w, up_w, down_w[0].T
    (out,) = ffn_part(at, 0, near.reshape(384, 2880), *hbm_weights)
    pairs = [after(pair, out)] + from_others(pair, "y")
    grads = local_grad(at, pairs, context)
    part = grads[0].astype(F32) + core_swap(grads[1]).astype(F32)
    terms = [shift("x", o, 4)(part[o].astype(BF)) for o in (1, 2, 3)]
    out, *weights = ffn_part(at, 1, far, *hbm_weights, out)
    terms = lax.optimization_barrier((*terms, out))[:3]
    total = part[0] + terms[0].astype(F32) + terms[1].astype(F32) + terms[2].astype(F32)
    rows = total.reshape(2, 720, 128)
    kept = lax.dynamic_index_in_dim(rows, zh, 0, keepdims=False)
    gone = lax.dynamic_index_in_dim(rows, 1 - zh, 0, keepdims=False).astype(BF)
    came = zh_swap(gone)
    (out,) = ffn_part(at, 2, far, *weights, after(out, gone))
    total = (kept + after(came, out).astype(F32)).astype(BF)
    full = lax.all_gather(after(total, out), ("x", "zh"), axis=0, tiled=True).reshape(4, 1440, 128)

    out = after(out, total).reshape(64, 24, 2880)
    out = lax.all_to_all(out, over + ("y",), split_axis=0, concat_axis=0, tiled=True)
    own, sib = combine(at, out.reshape(2, 768, 2880), mine[2880:], sibling[2880:], mine)
    full = after(full, own, sib)
    grad = spread(at, full, core_swap(full)).reshape(2880, 512)
    mixed = (own + core_swap(sib).astype(F32)).astype(BF)
    return mixed.T, grad.T


def solution(mesh):
    fine = Mesh(mesh.devices.reshape(4, 2, 2, 4, 2), ("x", "zh", "core", "y", "zl"))
    every = ("x", "zh", "core", "y", "zl")
    two, three = P(every, None), P(every, None, None)
    in_specs = (two, two, two, two, P(), three, three, three, P(("x", "zh", "core"), ("y", "zl")), two)
    out_specs = (two, P(("y", "zl"), None))
    return jax.shard_map(local, mesh=fine, in_specs=in_specs, out_specs=out_specs, check_vma=False)
```
